32 devices in a mesh: row: 4 (over y, x), col: 8 (over z, core).
Axes of the slice: x: 2, y: 2, z: 4, core: 2. Of those that a mesh axis runs over, the one named last changes fastest.
Arguments:
- amplitudes: bfloat16 [16, 768, 768], P('row', 'col'), may hold values from -6 to 6
- factors: bfloat16 [32, 768, 768], P('col', 'row'), may hold values from -0.109375 to 0.109375
- counts: int32 [4], replicated, may hold values from 1 to 4, 8 in all
- pair_index: int32 [16, 2], replicated, may hold values from 0 to 23
- occ_energy: float32 [24], replicated, may hold values from -2 to -0.5
- vir_energy: float32 [768], replicated, may hold values from 0.5 to 3
Outputs:
- new_amplitudes: bfloat16 [16, 768, 768], P('row', 'col')
The draws below stay inside these ranges and needn't reach their ends.
Inputs may be any that keep to these rules, and one draw needn't show every extreme that they name: The counts sum to 2 times the number of owner rows. `pair_index`: entries of slots that are not live are not used.
All inputs are finite; a program needn't handle non-finite values.
Results may differ from the reference program's by a relative error of at most 0.0046.
Values may be sent and summed in bfloat16 or wider, within the bound.
A program may use at most 64 MiB of HBM per device.

```python
import math
import jax
import jax.numpy as jnp
import numpy as np
from jax import lax

V = 768
NOCC = 24
WORK = 2
SLOTS = 4
NQ = 32
N_ROW = 4


def set_ends(array, rng, low, high):
    place = [jax.random.randint(jax.random.fold_in(rng, axis), (), 0, length) for axis, length in enumerate(array.shape)]
    main_axis = array.shape.index(max(array.shape))
    neighbour = place[:main_axis] + [(place[main_axis] + 1) % array.shape[main_axis]] + place[main_axis + 1:]
    return array.at[tuple(place)].set(low).at[tuple(neighbour)].set(high)


def levels(rng, dims, cuts, low, high):
    def one(position, shards_of):
        draws = jax.random.uniform(jax.random.fold_in(jax.random.fold_in(rng, 6), position), (shards_of,), jnp.float32, low / len(cuts), high / len(cuts))
        return jnp.repeat(jnp.exp(draws), dims[position] // shards_of).reshape((-1,) + (1,) * (len(dims) - position - 1))

    loudness = one(*cuts[0])
    for cut in cuts[1:]:
        loudness = loudness * one(*cut)
    return loudness


def profile(number_of, total, reach, lean):
    loads = [(1 << 20) // math.isqrt(grade ** lean) + 1 for grade in range(2, number_of + 1)]
    rest, given = total - reach - (number_of - 1), [1] * (number_of - 1)
    while rest > 0:
        movable = [i for i in range(number_of - 1) if given[i] < reach]
        mass, remaining = sum([loads[i] for i in movable]), rest
        for i in movable:
            addition = min(reach - given[i], max(1, remaining * loads[i] // mass), rest)
            given[i] = given[i] + addition
            rest = rest - addition
    return np.array([reach] + given)


def ragged(stream_key, number_of, total, bound, skew):
    if number_of == 2:
        one = jax.random.randint(stream_key, (), max(1, total - bound), min(bound, total - 1) + 1)
        return jnp.stack([one, total - one])
    tallies = jnp.asarray(profile(number_of, total, bound, skew), jnp.int32)
    couples = (number_of - 1) // 2
    source_of, receiver = tallies[1:1 + 2 * couples:2], tallies[2:2 + 2 * couples:2]
    margin = jnp.minimum(source_of - 1, bound - receiver)
    shifted = jax.random.randint(jax.random.fold_in(stream_key, 1), (couples,), 0, 1 << 20) % (margin + 1)
    tallies = tallies.at[1:1 + 2 * couples:2].set(source_of - shifted).at[2:2 + 2 * couples:2].set(receiver + shifted)
    return tallies[jax.random.permutation(jax.random.fold_in(stream_key, 2), number_of)]


def gaussian(own_key, dims, spread, most, split=(), kind=jnp.bfloat16):
    entries = jax.random.normal(own_key, dims, jnp.float32) * spread
    if len(split) > 0:
        entries = levels(own_key, dims, split, -0.22, 0.18) * entries
    return jnp.clip(entries, min=-most, max=most).astype(kind)


def setup_inputs(seed: int = 0) -> dict:
    keys = jax.random.split(jax.random.key(seed), 7)
    amplitudes = gaussian(keys[0], (N_ROW * SLOTS, V, V), 1.0, 6.0, ((0, 4), (1, 8)))
    factors = gaussian(keys[1], (NQ, V, V), (4 * V) ** -0.5, 0.109375, ((0, 8), (1, 4)))
    counts = ragged(keys[2], N_ROW, WORK * N_ROW, SLOTS, 2).astype(jnp.int32)
    pair_index = set_ends(jax.random.randint(keys[3], (N_ROW * SLOTS, 2), 0, NOCC), jax.random.fold_in(keys[3], 1), 0, NOCC - 1).astype(jnp.int32)
    occ_energy = jnp.clip(jax.random.uniform(keys[4], (NOCC,), jnp.float32, -2.0, -0.5), -2.0, -0.5)
    vir_energy = jnp.clip(jax.random.uniform(keys[5], (V,), jnp.float32, 0.5, 3.0), 0.5, 3.0)
    return {"amplitudes": amplitudes, "factors": factors, "counts": counts, "pair_index": pair_index, "occ_energy": occ_energy, "vir_energy": vir_energy}


level_shift = 1.0


def reference(amplitudes, factors, counts, pair_index, occ_energy, vir_energy):
    total_slots = amplitudes.shape[0]
    slot_ids = jnp.arange(total_slots, dtype=jnp.int32)
    owner_rows = slot_ids // SLOTS
    is_live = (slot_ids % SLOTS) < counts[owner_rows]
    pair_energy = occ_energy[pair_index[:, 0]] + occ_energy[pair_index[:, 1]]
    base = vir_energy[:, None] + vir_energy[None, :]
    factor_float = factors.astype(jnp.float32)

    def single_pair(packed):
        amps, energy, alive = packed
        amps_float = amps.astype(jnp.float32)
        halfway = jnp.einsum("cb,qdb->qcd", amps_float, factor_float).astype(jnp.bfloat16)
        ladder = jnp.einsum("qac,qcd->ad", factor_float, halfway.astype(jnp.float32))
        denominator = base - energy
        updated = amps_float - (ladder + denominator * amps_float) / (denominator + level_shift)
        return jnp.where(alive, updated, 0.0).astype(jnp.bfloat16)

    return lax.map(single_pair, (amplitudes, pair_energy, is_live))
```

```python
import functools

import jax
import jax.numpy as jnp
from jax import lax
from jax.experimental import pallas as pl
from jax.experimental.pallas import tpu as pltpu
from jax.sharding import PartitionSpec as P

WORK = 2
level_shift = 1.0
MESH = pl.DeviceIdType.MESH


def rank_range(pos, n, slots):
    total = WORK * n
    if isinstance(pos, int):
        return max(pos, total - slots * (n - pos)), min(slots * (pos + 1), total - (n - pos - 1))
    low = jnp.maximum(pos, total - slots * (n - pos))
    high = jnp.minimum(slots * (pos + 1), total - (n - pos - 1))
    return low, high


def reach_of(n, slots):
    reach = 0
    for pos in range(n):
        low, high = rank_range(pos, n, slots)
        reach = max([reach] + [abs(k // WORK - pos) for k in range(low, high)])
    return reach


def kernel(n, m, reach, amps, factors, counts, pairs, occ, vir, out,
           full, held, half, acc, stage, shuf, sib_out, sib_in, z_out, z_in, ret,
           l_send, l_recv, s_send, s_recv, t_send, t_recv, f_send, f_recv,
           b_send, b_recv, z_send, z_recv, r_send, r_recv):
    slots, rows, size = amps.shape
    vectors, block = factors.shape[0], factors.shape[1]
    nz = m // 2
    row, col = lax.axis_index("row"), lax.axis_index("col")
    z, core = col // 2, col % 2
    sibling = z * 2 + 1 - core
    pos = row // 2 + (row % 2) * (n - 1 - 2 * (row // 2))

    def row_at(p):
        if isinstance(p, int):
            return 2 * p if p < n // 2 else 2 * (n - 1 - p) + 1
        back = p // (n // 2)
        return (1 - back) * 2 * p + back * (2 * (n - 1 - p) + 1)

    def remote(src, dst, send, recv, **where):
        return pltpu.make_async_remote_copy(
            src_ref=src, dst_ref=dst, send_sem=send, recv_sem=recv, device_id=where, device_id_type=MESH)

    barrier = pltpu.get_barrier_semaphore()
    for step in range(1, n):
        pl.semaphore_signal(barrier, inc=1, device_id={"row": (row + step) % n}, device_id_type=MESH)
    for step in range(1, m):
        pl.semaphore_signal(barrier, inc=1, device_id={"col": (col + step) % m}, device_id_type=MESH)

    count_at = [counts[row_at(p)] for p in range(n)]
    start_at, running = [], jnp.int32(0)
    for p in range(n):
        start_at.append(running)
        running = running + count_at[p]

    def lookup(values, p):
        found = jnp.int32(0)
        for i in range(n):
            found = jnp.where(p == i, values[i], found)
        return found

    own_start, own_count = lookup(start_at, pos), lookup(count_at, pos)

    def owner_of(rank):
        src = jnp.int32(0)
        for p in range(n - 1):
            src = src + jnp.where(start_at[p] + count_at[p] <= rank, 1, 0)
        return src

    def feasible(p, worker, j):
        low, high = rank_range(p, n, slots)
        rank = worker * WORK + j
        return (p >= 0) & (p < n) & (worker >= 0) & (worker < n) & (rank >= low) & (rank < high)

    shifts = [d for d in range(-reach, reach + 1) if d != 0]
    for j in range(WORK):
        for d in shifts:
            slot = jnp.clip((pos + d) * WORK + j - own_start, 0, slots - 1)
            stage[d + reach, j] = amps[slot]
        shuf[reach, j] = amps[jnp.clip(pos * WORK + j - own_start, 0, slots - 1)]

    pl.semaphore_wait(barrier, n + m - 2)

    def shuffle(j, d):
        target = row_at((pos + d + n) % n)
        return remote(stage.at[d + reach, j], shuf.at[reach - d, j], s_send.at[d + reach, j], s_recv.at[reach - d, j],
                      row=target)

    def give_back(j, d):
        target = row_at((pos + d + n) % n)
        return remote(ret.at[reach, j], ret.at[reach - d, j], r_send.at[d + reach, j], r_recv.at[reach - d, j],
                      row=target)

    for j in range(WORK):
        for d in shifts:
            pl.when(feasible(pos, pos + d, j))(lambda j=j, d=d: shuffle(j, d).start())

    steps = n // 2
    part = block // 2

    def ring(step, q, way):
        move = 1 if way == 0 else -1
        origin = row_at((pos - move * step + n) % n)
        target = row_at((pos + move + n) % n)
        src = factors.at[q] if step == 0 else full.at[q, origin]
        dst = full.at[q, origin]
        if step == steps - 1:
            cut = pl.ds(way * part, part)
            src, dst = src.at[cut], dst.at[cut]
        return remote(src, dst, l_send.at[way, step, q], l_recv.at[way, step, q], row=target)

    def group(t):
        for step in range(steps - 1, -1, -1):
            q = t - 2 * step
            if 0 <= q < vectors:
                for way in range(2):
                    if step > 0:
                        ring(step - 1, q, way).wait_recv()
                    ring(step, q, way).start()

    groups = vectors + 2 * (steps - 1)
    ahead = 2 * (steps - 1)
    for t in range(min(2, groups)):
        group(t)

    def own_block(q, _):
        full[q, row] = factors[q]
        return 0

    lax.fori_loop(0, vectors, own_block, 0)

    def along(j, o):
        return remote(held.at[j, col], held.at[j, col], t_send.at[j, o], t_recv.at[j, o],
                      col=((z + o) % nz) * 2 + core)

    def across(j, o):
        from_z = (z - o + nz) % nz
        src = from_z * 2 + core
        return remote(held.at[j, src], held.at[j, src], f_send.at[j, o], f_recv.at[j, o], col=sibling)

    for j in range(WORK):
        for d in shifts:
            pl.when(feasible(pos - d, pos, j))(lambda j=j, d=d: shuffle(j, d).wait_recv())
        src = owner_of(pos * WORK + j) - pos
        chosen = shuf[reach, j]
        for d in shifts:
            chosen = jnp.where(src == d, shuf[d + reach, j], chosen)
        held[j, col] = chosen
        for o in range(1, nz):
            along(j, o).start()
        across(j, 0).start()

    for t in range(2, min(ahead + 1, groups)):
        group(t)
    for j in range(WORK):
        for o in range(1, nz):
            along(j, o).wait_recv()
            across(j, o).start()
    if ahead + 1 < groups:
        group(ahead + 1)

    tile = size // 2

    def pair_step(q, j):
        def first(i, _):
            at = pl.ds(pl.multiple_of(i * tile, tile), tile)
            lhs = held.at[j].reshape(size, size)[at, :]
            rhs = full[q].reshape(size, size)
            half[at, :] = lax.dot_general(
                lhs, rhs, (((1,), (1,)), ((), ())), preferred_element_type=jnp.float32).astype(jnp.bfloat16)
            return 0

        def second(i, _):
            at = pl.ds(pl.multiple_of(i * tile, tile), tile)
            lhs = full.at[q].reshape(size, size)[at, :]
            value = jnp.dot(lhs, half[...], preferred_element_type=jnp.float32)
            if q == 0:
                acc[j, at, :] = value
            else:
                acc[j, at, :] += value
            return 0

        lax.fori_loop(0, size // tile, first, 0)
        lax.fori_loop(0, size // tile, second, 0)

    def rows_of(c):
        return pl.ds(pl.multiple_of(c * rows, rows), rows)

    def to_sibling(j):
        return remote(sib_out.at[j], sib_in.at[j], b_send.at[j], b_recv.at[j], col=sibling)

    def to_owner(j, o):
        return remote(z_out.at[j, o], z_in.at[j, o], z_send.at[j, o], z_recv.at[j, o],
                      col=((z + o) % nz) * 2 + core)

    def share(j):
        for k in range(nz):
            sib_out[j, k] = acc[j, rows_of(2 * k + 1 - core), :].astype(jnp.bfloat16)
        to_sibling(j).start()

    def spread(j):
        to_sibling(j).wait_recv()
        for o in range(1, nz):
            k = (z + o) % nz
            total = acc[j, rows_of(2 * k + core), :] + sib_in[j, k].astype(jnp.float32)
            z_out[j, o] = total.astype(jnp.bfloat16)
            to_owner(j, o).start()

    def finish(j):
        rank = pos * WORK + j
        src = owner_of(rank)
        slot = rank - lookup(start_at, src)
        pair = jnp.clip(lookup([row_at(p) for p in range(n)], src) * slots + slot, 0, n * slots - 1)
        energy = occ[pairs[pair, 0]] + occ[pairs[pair, 1]]
        here = lax.broadcasted_iota(jnp.int32, (rows, size), 0) + col * rows
        there = lax.broadcasted_iota(jnp.int32, (rows, size), 1)
        levels = jnp.broadcast_to(vir[...], (rows, size))
        mine = jnp.sum(jnp.where(here == there, levels, 0.0), axis=1, keepdims=True)
        denominator = mine + levels - energy
        ladder = acc[j, rows_of(col), :] + sib_in[j, z].astype(jnp.float32)
        for o in range(1, nz):
            to_owner(j, o).wait_recv()
            ladder = ladder + z_in[j, o].astype(jnp.float32)
        t = held[j, col].astype(jnp.float32)
        new = t - (ladder + denominator * t) / (denominator + level_shift)
        ret[reach, j] = new.astype(jnp.bfloat16)
        for d in shifts:
            pl.when(feasible(pos + d, pos, j))(lambda j=j, d=d: give_back(j, d).start())

    for q in range(vectors):
        t = q + ahead + 1
        if q > 0 and t < groups:
            group(t)
        for way in range(2):
            ring(steps - 1, q, way).wait_recv()
        for j in range(WORK):
            if q == 0:
                for o in range(nz):
                    across(j, o).wait_recv()
            pair_step(q, j)
            if q == vectors - 1:
                share(j)
                if j > 0:
                    spread(j - 1)
    spread(WORK - 1)
    for j in range(WORK):
        finish(j)
    for j in range(WORK):
        for d in shifts:
            pl.when(feasible(pos, pos + d, j))(lambda j=j, d=d: give_back(j, -d).wait_recv())
    for s in range(slots):
        rank = own_start + s
        where = jnp.clip(rank // WORK - pos + reach, 0, 2 * reach)
        value = ret[where, jnp.clip(rank % WORK, 0, WORK - 1)]
        out[s] = jnp.where(s < own_count, value, jnp.zeros_like(value))

    for j in range(WORK):
        for d in shifts:
            pl.when(feasible(pos, pos + d, j))(lambda j=j, d=d: shuffle(j, d).wait_send())
            pl.when(feasible(pos + d, pos, j))(lambda j=j, d=d: give_back(j, d).wait_send())
        for o in range(1, nz):
            along(j, o).wait_send()
            to_owner(j, o).wait_send()
        for o in range(nz):
            across(j, o).wait_send()
        to_sibling(j).wait_send()
    for q in range(vectors):
        for step in range(steps):
            for way in range(2):
                ring(step, q, way).wait_send()


def solution(mesh):
    n, m = mesh.shape["row"], mesh.shape["col"]

    def per_device(amplitudes, factors, counts, pair_index, occ_energy, vir_energy):
        slots, rows, size = amplitudes.shape
        vectors, block, _ = factors.shape
        reach = reach_of(n, slots)
        span, nz, steps = 2 * reach + 1, m // 2, n // 2
        bf16, f32 = jnp.bfloat16, jnp.float32
        dma = pltpu.SemaphoreType.DMA
        vmem, smem = pl.BlockSpec(memory_space=pltpu.VMEM), pl.BlockSpec(memory_space=pltpu.SMEM)
        flops = 4 * vectors * WORK * size ** 3
        return pl.pallas_call(
            functools.partial(kernel, n, m, reach),
            out_shape=jax.ShapeDtypeStruct((slots, rows, size), bf16),
            in_specs=[vmem, vmem, smem, smem, smem, vmem],
            out_specs=vmem,
            scratch_shapes=[
                pltpu.VMEM((vectors, n, block, size), bf16),
                pltpu.VMEM((WORK, m, rows, size), bf16),
                pltpu.VMEM((size, size), bf16),
                pltpu.VMEM((WORK, size, size), f32),
                pltpu.VMEM((span, WORK, rows, size), bf16),
                pltpu.VMEM((span, WORK, rows, size), bf16),
                pltpu.VMEM((WORK, nz, rows, size), bf16),
                pltpu.VMEM((WORK, nz, rows, size), bf16),
                pltpu.VMEM((WORK, nz, rows, size), bf16),
                pltpu.VMEM((WORK, nz, rows, size), bf16),
                pltpu.VMEM((span, WORK, rows, size), bf16),
                dma((2, steps, vectors)), dma((2, steps, vectors)),
                dma((span, WORK)), dma((span, WORK)),
                dma((WORK, nz)), dma((WORK, nz)),
                dma((WORK, nz)), dma((WORK, nz)),
                dma((WORK,)), dma((WORK,)),
                dma((WORK, nz)), dma((WORK, nz)),
                dma((span, WORK)), dma((span, WORK)),
            ],
            cost_estimate=pl.CostEstimate(flops=flops, bytes_accessed=2 * vectors * size * size, transcendentals=0),
            compiler_params=pltpu.CompilerParams(
                collective_id=0, has_side_effects=True, vmem_limit_bytes=56 * 2 ** 20),
        )(amplitudes, factors, counts, pair_index, occ_energy, vir_energy.reshape(1, size))

    in_specs = (P("row", "col", None), P("col", "row", None), P(), P(), P(), P())
    return jax.shard_map(
        per_device, mesh=mesh, in_specs=in_specs, out_specs=P("row", "col", None), check_vma=False)
```

```python
import functools

import jax
import jax.numpy as jnp
from jax import lax
from jax.experimental import pallas as pl
from jax.experimental.pallas import tpu as pltpu
from jax.sharding import PartitionSpec as P

WORK = 2
level_shift = 1.0
MESH = pl.DeviceIdType.MESH


def rank_range(pos, n, slots):
    total = WORK * n
    if isinstance(pos, int):
        return max(pos, total - slots * (n - pos)), min(slots * (pos + 1), total - (n - pos - 1))
    low = jnp.maximum(pos, total - slots * (n - pos))
    high = jnp.minimum(slots * (pos + 1), total - (n - pos - 1))
    return low, high


def reach_of(n, slots):
    reach = 0
    for pos in range(n):
        low, high = rank_range(pos, n, slots)
        reach = max([reach] + [abs(k // WORK - pos) for k in range(low, high)])
    return reach


def kernel(n, m, reach, amps, factors, counts, pairs, occ, vir, out,
           full, held, half, acc, stage, shuf, sib_out, sib_in, z_out, z_in, ret,
           l_send, l_recv, s_send, s_recv, t_send, t_recv, f_send, f_recv,
           b_send, b_recv, z_send, z_recv, r_send, r_recv):
    slots, rows, size = amps.shape
    vectors, block = factors.shape[0], factors.shape[1]
    nz = m // 2
    row, col = lax.axis_index("row"), lax.axis_index("col")
    z, core = col // 2, col % 2
    sibling = z * 2 + 1 - core
    pos = row // 2 + (row % 2) * (n - 1 - 2 * (row // 2))

    def row_at(p):
        if isinstance(p, int):
            return 2 * p if p < n // 2 else 2 * (n - 1 - p) + 1
        back = p // (n // 2)
        return (1 - back) * 2 * p + back * (2 * (n - 1 - p) + 1)

    def remote(src, dst, send, recv, **where):
        return pltpu.make_async_remote_copy(
            src_ref=src, dst_ref=dst, send_sem=send, recv_sem=recv, device_id=where, device_id_type=MESH)

    barrier = pltpu.get_barrier_semaphore()
    for step in range(1, n):
        pl.semaphore_signal(barrier, inc=1, device_id={"row": (row + step) % n}, device_id_type=MESH)
    for step in range(1, m):
        pl.semaphore_signal(barrier, inc=1, device_id={"col": (col + step) % m}, device_id_type=MESH)

    count_at = [counts[row_at(p)] for p in range(n)]
    start_at, running = [], jnp.int32(0)
    for p in range(n):
        start_at.append(running)
        running = running + count_at[p]

    def lookup(values, p):
        found = jnp.int32(0)
        for i in range(n):
            found = jnp.where(p == i, values[i], found)
        return found

    own_start, own_count = lookup(start_at, pos), lookup(count_at, pos)

    def owner_of(rank):
        src = jnp.int32(0)
        for p in range(n - 1):
            src = src + jnp.where(start_at[p] + count_at[p] <= rank, 1, 0)
        return src

    def feasible(p, worker, j):
        low, high = rank_range(p, n, slots)
        rank = worker * WORK + j
        return (p >= 0) & (p < n) & (worker >= 0) & (worker < n) & (rank >= low) & (rank < high)

    shifts = [d for d in range(-reach, reach + 1) if d != 0]
    for j in range(WORK):
        for d in shifts:
            slot = jnp.clip((pos + d) * WORK + j - own_start, 0, slots - 1)
            stage[d + reach, j] = amps[slot]
        shuf[reach, j] = amps[jnp.clip(pos * WORK + j - own_start, 0, slots - 1)]

    pl.semaphore_wait(barrier, n + m - 2)

    def shuffle(j, d):
        target = row_at((pos + d + n) % n)
        return remote(stage.at[d + reach, j], shuf.at[reach - d, j], s_send.at[d + reach, j], s_recv.at[reach - d, j],
                      row=target)

    def give_back(j, d):
        target = row_at((pos + d + n) % n)
        return remote(ret.at[reach, j], ret.at[reach - d, j], r_send.at[d + reach, j], r_recv.at[reach - d, j],
                      row=target)

    for j in range(WORK):
        for d in shifts:
            pl.when(feasible(pos, pos + d, j))(lambda j=j, d=d: shuffle(j, d).start())

    steps = n // 2
    part = block // 2

    def ring(step, q, way):
        move = 1 if way == 0 else -1
        origin = row_at((pos - move * step + n) % n)
        target = row_at((pos + move + n) % n)
        src = factors.at[q] if step == 0 else full.at[q, origin]
        dst = full.at[q, origin]
        if step == steps - 1:
            cut = pl.ds(way * part, part)
            src, dst = src.at[cut], dst.at[cut]
        return remote(src, dst, l_send.at[way, step, q], l_recv.at[way, step, q], row=target)

    def group(t):
        for step in range(steps - 1, -1, -1):
            q = t - 2 * step
            if 0 <= q < vectors:
                for way in range(2):
                    if step > 0:
                        ring(step - 1, q, way).wait_recv()
                    ring(step, q, way).start()

    groups = vectors + 2 * (steps - 1)
    ahead = 2 * (steps - 1)
    for t in range(min(2, groups)):
        group(t)

    def own_block(q, _):
        full[q, row] = factors[q]
        return 0

    lax.fori_loop(0, vectors, own_block, 0)

    def passed(h, way):
        return z - h if way == 0 else z + h

    def arrives(h, way):
        return passed(h + 1, way) >= 0 if way == 0 else passed(h + 1, way) < nz

    def leaves(h, way):
        there = passed(h, way) >= 0 if way == 0 else passed(h, way) < nz
        return there & (z + 1 < nz if way == 0 else z > 0)

    def along(j, h, way):
        src = passed(h, way) * 2 + core
        target = (jnp.minimum(z + 1, nz - 1) if way == 0 else jnp.maximum(z - 1, 0)) * 2 + core
        return remote(held.at[j, src], held.at[j, src], t_send.at[j, way, h], t_recv.at[j, way, h], col=target)

    def across(j, h, way):
        src = passed(h, way) * 2 + core
        return remote(held.at[j, src], held.at[j, src], f_send.at[j, way, h], f_recv.at[j, way, h], col=sibling)

    def hop(j, h, way):
        @pl.when(arrives(h - 1, way))
        def _():
            along(j, h - 1, way).wait_recv()
            if h < nz - 1:
                pl.when(leaves(h, way))(lambda: along(j, h, way).start())
            across(j, h, way).start()

    for j in range(WORK):
        for d in shifts:
            pl.when(feasible(pos - d, pos, j))(lambda j=j, d=d: shuffle(j, d).wait_recv())
        src = owner_of(pos * WORK + j) - pos
        chosen = shuf[reach, j]
        for d in shifts:
            chosen = jnp.where(src == d, shuf[d + reach, j], chosen)
        held[j, col] = chosen
        for way in range(2):
            pl.when(leaves(0, way))(lambda j=j, way=way: along(j, 0, way).start())
        across(j, 0, 0).start()

    later = list(range(2, min(ahead + 2, groups)))
    for h in range(1, nz):
        for j in range(WORK):
            for way in range(2):
                hop(j, h, way)
        if later:
            group(later.pop(0))
    for t in later:
        group(t)

    tile = size // 2

    def pair_first(q, j):
        def first(i, _):
            at = pl.ds(pl.multiple_of(i * tile, tile), tile)
            lhs = held.at[j].reshape(size, size)[at, :]
            rhs = full[q].reshape(size, size)
            half[at, :] = lax.dot_general(
                lhs, rhs, (((1,), (1,)), ((), ())), preferred_element_type=jnp.float32).astype(jnp.bfloat16)
            return 0

        lax.fori_loop(0, size // tile, first, 0)

    def pair_second(q, j):
        def second(i, _):
            at = pl.ds(pl.multiple_of(i * tile, tile), tile)
            lhs = full.at[q].reshape(size, size)[at, :]
            value = jnp.dot(lhs, half[...], preferred_element_type=jnp.float32)
            if q == 0:
                acc[j, at, :] = value
            else:
                acc[j, at, :] += value
            return 0

        lax.fori_loop(0, size // tile, second, 0)

    def rows_of(c):
        return pl.ds(pl.multiple_of(c * rows, rows), rows)

    def to_sibling(j):
        return remote(sib_out.at[j], sib_in.at[j], b_send.at[j], b_recv.at[j], col=sibling)

    def onward(j, k, way):
        target = (jnp.minimum(z + 1, nz - 1) if way == 0 else jnp.maximum(z - 1, 0)) * 2 + core
        slot = k if way == 0 else jnp.where(k == z - 1, nz, k)
        return remote(z_out.at[j, k], z_in.at[j, slot], z_send.at[j, k], z_recv.at[j, slot], col=target)

    def incoming(j, slot):
        sent = min(slot, nz - 1) if isinstance(slot, int) else slot
        return remote(z_out.at[j, sent], z_in.at[j, slot], z_send.at[j, sent], z_recv.at[j, slot], col=sibling)

    def share(j):
        for k in range(nz):
            sib_out[j, k] = acc[j, rows_of(2 * k + 1 - core), :].astype(jnp.bfloat16)
        to_sibling(j).start()

    def chain(j, action):
        for i in range(nz - 1):
            for way in range(2):
                k = nz - 1 - i if way == 0 else i
                ahead_of = (k > z) if way == 0 else (k < z)
                first = (z == 0) if way == 0 else (z == nz - 1)
                action(j, k, way, ahead_of, first)

    def begin(j, k, way, ahead_of, first):
        @pl.when(ahead_of & first)
        def _():
            total = acc[j, rows_of(2 * k + core), :] + sib_in[j, k].astype(jnp.float32)
            z_out[j, k] = total.astype(jnp.bfloat16)
            onward(j, k, way).start()

    def go_on(j, k, way, ahead_of, first):
        @pl.when(ahead_of & jnp.logical_not(first))
        def _():
            total = acc[j, rows_of(2 * k + core), :] + sib_in[j, k].astype(jnp.float32)
            incoming(j, k).wait_recv()
            z_out[j, k] = (total + z_in[j, k].astype(jnp.float32)).astype(jnp.bfloat16)
            onward(j, k, way).start()

    def spread(j):
        to_sibling(j).wait_recv()
        chain(j, begin)

    def finish(j):
        rank = pos * WORK + j
        src = owner_of(rank)
        slot = rank - lookup(start_at, src)
        pair = jnp.clip(lookup([row_at(p) for p in range(n)], src) * slots + slot, 0, n * slots - 1)
        energy = occ[pairs[0, pair]] + occ[pairs[1, pair]]
        here = lax.broadcasted_iota(jnp.int32, (rows, size), 0) + col * rows
        there = lax.broadcasted_iota(jnp.int32, (rows, size), 1)
        levels = jnp.broadcast_to(vir[...], (rows, size))
        mine = jnp.sum(jnp.where(here == there, levels, 0.0), axis=1, keepdims=True)
        denominator = mine + levels - energy
        own = rows_of(col)
        acc[j, own, :] += sib_in[j, z].astype(jnp.float32)

        @pl.when(z > 0)
        def _():
            incoming(j, z).wait_recv()
            acc[j, own, :] += z_in[j, z].astype(jnp.float32)

        @pl.when(z < nz - 1)
        def _():
            incoming(j, nz).wait_recv()
            acc[j, own, :] += z_in[j, nz].astype(jnp.float32)

        ladder = acc[j, own, :]
        t = held[j, col].astype(jnp.float32)
        new = t - (ladder + denominator * t) / (denominator + level_shift)
        ret[reach, j] = new.astype(jnp.bfloat16)
        for d in shifts:
            pl.when(feasible(pos + d, pos, j))(lambda j=j, d=d: give_back(j, d).start())

    for q in range(vectors):
        t = q + ahead + 1
        if q > 0 and t < groups:
            group(t)
        for way in range(2):
            ring(steps - 1, q, way).wait_recv()
        for j in range(WORK):
            if q == 0:
                across(j, 0, 0).wait_recv()
                for h in range(1, nz):
                    for way in range(2):
                        pl.when(arrives(h - 1, way))(lambda j=j, h=h, way=way: across(j, h, way).wait_recv())
            pair_first(q, j)
            if q == vectors - 1 and j > 0:
                spread(j - 1)
            pair_second(q, j)
            if q == vectors - 1:
                share(j)
    for j in range(WORK - 1):
        chain(j, go_on)
    spread(WORK - 1)
    for j in range(WORK - 1):
        finish(j)
    chain(WORK - 1, go_on)
    finish(WORK - 1)
    for j in range(WORK):
        for d in shifts:
            pl.when(feasible(pos, pos + d, j))(lambda j=j, d=d: give_back(j, -d).wait_recv())
    for s in range(slots):
        rank = own_start + s
        where = jnp.clip(rank // WORK - pos + reach, 0, 2 * reach)
        value = ret[where, jnp.clip(rank % WORK, 0, WORK - 1)]
        out[s] = jnp.where(s < own_count, value, jnp.zeros_like(value))

    for j in range(WORK):
        for d in shifts:
            pl.when(feasible(pos, pos + d, j))(lambda j=j, d=d: shuffle(j, d).wait_send())
            pl.when(feasible(pos + d, pos, j))(lambda j=j, d=d: give_back(j, d).wait_send())
        across(j, 0, 0).wait_send()
        for way in range(2):
            for h in range(nz - 1):
                pl.when(leaves(h, way))(lambda j=j, h=h, way=way: along(j, h, way).wait_send())
                pl.when(arrives(h, way))(lambda j=j, h=h, way=way: across(j, h + 1, way).wait_send())
        for k in range(nz):
            pl.when(z != k)(lambda j=j, k=k: incoming(j, k).wait_send())
        to_sibling(j).wait_send()
    for q in range(vectors):
        for step in range(steps):
            for way in range(2):
                ring(step, q, way).wait_send()


def solution(mesh):
    n, m = mesh.shape["row"], mesh.shape["col"]

    def per_device(amplitudes, factors, counts, pair_index, occ_energy, vir_energy):
        slots, rows, size = amplitudes.shape
        vectors, block, _ = factors.shape
        reach = reach_of(n, slots)
        span, nz, steps = 2 * reach + 1, m // 2, n // 2
        bf16, f32 = jnp.bfloat16, jnp.float32
        dma = pltpu.SemaphoreType.DMA
        vmem, smem = pl.BlockSpec(memory_space=pltpu.VMEM), pl.BlockSpec(memory_space=pltpu.SMEM)
        flops = 4 * vectors * WORK * size ** 3
        return pl.pallas_call(
            functools.partial(kernel, n, m, reach),
            out_shape=jax.ShapeDtypeStruct((slots, rows, size), bf16),
            in_specs=[vmem, vmem, smem, smem, smem, vmem],
            out_specs=vmem,
            scratch_shapes=[
                pltpu.VMEM((vectors, n, block, size), bf16),
                pltpu.VMEM((WORK, m, rows, size), bf16),
                pltpu.VMEM((size, size), bf16),
                pltpu.VMEM((WORK, size, size), f32),
                pltpu.VMEM((span, WORK, rows, size), bf16),
                pltpu.VMEM((span, WORK, rows, size), bf16),
                pltpu.VMEM((WORK, nz, rows, size), bf16),
                pltpu.VMEM((WORK, nz, rows, size), bf16),
                pltpu.VMEM((WORK, nz, rows, size), bf16),
                pltpu.VMEM((WORK, nz + 1, rows, size), bf16),
                pltpu.VMEM((span, WORK, rows, size), bf16),
                dma((2, steps, vectors)), dma((2, steps, vectors)),
                dma((span, WORK)), dma((span, WORK)),
                dma((WORK, 2, nz)), dma((WORK, 2, nz)),
                dma((WORK, 2, nz)), dma((WORK, 2, nz)),
                dma((WORK,)), dma((WORK,)),
                dma((WORK, nz)), dma((WORK, nz + 1)),
                dma((span, WORK)), dma((span, WORK)),
            ],
            cost_estimate=pl.CostEstimate(flops=flops, bytes_accessed=2 * vectors * size * size, transcendentals=0),
            compiler_params=pltpu.CompilerParams(
                collective_id=0, has_side_effects=True, vmem_limit_bytes=56 * 2 ** 20),
        )(amplitudes, factors, counts, pair_index.T, occ_energy, vir_energy)

    in_specs = (P("row", "col", None), P("col", "row", None), P(), P(), P(), P())
    return jax.shard_map(
        per_device, mesh=mesh, in_specs=in_specs, out_specs=P("row", "col", None), check_vma=False)
```

```python
import functools

import jax
import jax.numpy as jnp
from jax import lax
from jax.experimental import pallas as pl
from jax.experimental.pallas import tpu as pltpu
from jax.sharding import PartitionSpec as P

WORK = 2
level_shift = 1.0
MESH = pl.DeviceIdType.MESH


def rank_range(pos, n, slots):
    total = WORK * n
    if isinstance(pos, int):
        return max(pos, total - slots * (n - pos)), min(slots * (pos + 1), total - (n - pos - 1))
    low = jnp.maximum(pos, total - slots * (n - pos))
    high = jnp.minimum(slots * (pos + 1), total - (n - pos - 1))
    return low, high


def reach_of(n, slots):
    reach = 0
    for pos in range(n):
        low, high = rank_range(pos, n, slots)
        reach = max([reach] + [abs(k // WORK - pos) for k in range(low, high)])
    return reach


def kernel(n, m, reach, amps, factors, counts, pairs, occ, vir, out,
           full, held, half, acc, stage, shuf, sib_out, sib_in, z_out, z_in, ret,
           l_send, l_recv, s_send, s_recv, t_send, t_recv, f_send, f_recv,
           b_send, b_recv, z_send, z_recv, r_send, r_recv):
    slots, rows, size = amps.shape
    vectors, block = factors.shape[0], factors.shape[1]
    nz = m // 2
    row, col = lax.axis_index("row"), lax.axis_index("col")
    z, core = col // 2, col % 2
    sibling = z * 2 + 1 - core
    pos = row // 2 + (row % 2) * (n - 1 - 2 * (row // 2))

    def row_at(p):
        if isinstance(p, int):
            return 2 * p if p < n // 2 else 2 * (n - 1 - p) + 1
        back = p // (n // 2)
        return (1 - back) * 2 * p + back * (2 * (n - 1 - p) + 1)

    def remote(src, dst, send, recv, **where):
        return pltpu.make_async_remote_copy(
            src_ref=src, dst_ref=dst, send_sem=send, recv_sem=recv, device_id=where, device_id_type=MESH)

    barrier = pltpu.get_barrier_semaphore()
    for step in range(1, n):
        pl.semaphore_signal(barrier, inc=1, device_id={"row": (row + step) % n}, device_id_type=MESH)
    for step in range(1, m):
        pl.semaphore_signal(barrier, inc=1, device_id={"col": (col + step) % m}, device_id_type=MESH)

    count_at = [counts[row_at(p)] for p in range(n)]
    start_at, running = [], jnp.int32(0)
    for p in range(n):
        start_at.append(running)
        running = running + count_at[p]

    def lookup(values, p):
        found = jnp.int32(0)
        for i in range(n):
            found = jnp.where(p == i, values[i], found)
        return found

    own_start, own_count = lookup(start_at, pos), lookup(count_at, pos)

    def owner_of(rank):
        src = jnp.int32(0)
        for p in range(n - 1):
            src = src + jnp.where(start_at[p] + count_at[p] <= rank, 1, 0)
        return src

    def feasible(p, worker, j):
        low, high = rank_range(p, n, slots)
        rank = worker * WORK + j
        return (p >= 0) & (p < n) & (worker >= 0) & (worker < n) & (rank >= low) & (rank < high)

    shifts = [d for d in range(-reach, reach + 1) if d != 0]
    for j in range(WORK):
        for d in shifts:
            slot = jnp.clip((pos + d) * WORK + j - own_start, 0, slots - 1)
            stage[d + reach, j] = amps[slot]
        shuf[reach, j] = amps[jnp.clip(pos * WORK + j - own_start, 0, slots - 1)]

    pl.semaphore_wait(barrier, n + m - 2)

    def shuffle(j, d):
        target = row_at((pos + d + n) % n)
        return remote(stage.at[d + reach, j], shuf.at[reach - d, j], s_send.at[d + reach, j], s_recv.at[reach - d, j],
                      row=target)

    def give_back(j, d):
        target = row_at((pos + d + n) % n)
        return remote(ret.at[reach, j], ret.at[reach - d, j], r_send.at[d + reach, j], r_recv.at[reach - d, j],
                      row=target)

    for j in range(WORK):
        for d in shifts:
            pl.when(feasible(pos, pos + d, j))(lambda j=j, d=d: shuffle(j, d).start())

    steps = n // 2
    part = block // 2
    lead = 3

    def ring(step, q, way):
        move = 1 if way == 0 else -1
        origin = row_at((pos - move * step + n) % n)
        target = row_at((pos + move + n) % n)
        src = factors.at[q] if step == 0 else full.at[q, origin]
        dst = full.at[q, origin]
        if step == steps - 1:
            cut = pl.ds(way * part, part)
            src, dst = src.at[cut], dst.at[cut]
        return remote(src, dst, l_send.at[way, step, q], l_recv.at[way, step, q], row=target)

    def group(t):
        for step in range(steps - 1, -1, -1):
            q = t - lead * step
            if 0 <= q < vectors:
                for way in range(2):
                    if step > 0:
                        ring(step - 1, q, way).wait_recv()
                    ring(step, q, way).start()

    groups = vectors + lead * (steps - 1)
    ahead = lead * (steps - 1)
    for t in range(min(lead, groups)):
        group(t)

    def own_block(q, _):
        full[q, row] = factors[q]
        return 0

    lax.fori_loop(0, vectors, own_block, 0)

    def passed(h, way):
        return z - h if way == 0 else z + h

    def arrives(h, way):
        return passed(h + 1, way) >= 0 if way == 0 else passed(h + 1, way) < nz

    def leaves(h, way):
        there = passed(h, way) >= 0 if way == 0 else passed(h, way) < nz
        return there & (z + 1 < nz if way == 0 else z > 0)

    def along(j, h, way):
        src = passed(h, way) * 2 + core
        target = (jnp.minimum(z + 1, nz - 1) if way == 0 else jnp.maximum(z - 1, 0)) * 2 + core
        return remote(held.at[j, src], held.at[j, src], t_send.at[j, way, h], t_recv.at[j, way, h], col=target)

    def across(j, h, way):
        src = passed(h, way) * 2 + core
        return remote(held.at[j, src], held.at[j, src], f_send.at[j, way, h], f_recv.at[j, way, h], col=sibling)

    def hop(j, h, way):
        @pl.when(arrives(h - 1, way))
        def _():
            along(j, h - 1, way).wait_recv()
            if h < nz - 1:
                pl.when(leaves(h, way))(lambda: along(j, h, way).start())
            across(j, h, way).start()

    for j in range(WORK):
        for d in shifts:
            pl.when(feasible(pos - d, pos, j))(lambda j=j, d=d: shuffle(j, d).wait_recv())
        src = owner_of(pos * WORK + j) - pos
        chosen = shuf[reach, j]
        for d in shifts:
            chosen = jnp.where(src == d, shuf[d + reach, j], chosen)
        held[j, col] = chosen
        for way in range(2):
            pl.when(leaves(0, way))(lambda j=j, way=way: along(j, 0, way).start())
        across(j, 0, 0).start()

    later = list(range(lead, min(ahead + 2, groups)))
    for h in range(1, nz):
        for j in range(WORK):
            for way in range(2):
                hop(j, h, way)
        if later and h > 1:
            group(later.pop(0))
    for t in later:
        group(t)

    tile = size // 2

    def pair_first(q, j):
        def first(i, _):
            at = pl.ds(pl.multiple_of(i * tile, tile), tile)
            lhs = held.at[j].reshape(size, size)[at, :]
            rhs = full[q].reshape(size, size)
            half[at, :] = lax.dot_general(
                lhs, rhs, (((1,), (1,)), ((), ())), preferred_element_type=jnp.float32).astype(jnp.bfloat16)
            return 0

        lax.fori_loop(0, size // tile, first, 0)

    def pair_second(q, j):
        def second(i, _):
            at = pl.ds(pl.multiple_of(i * tile, tile), tile)
            lhs = full.at[q].reshape(size, size)[at, :]
            value = jnp.dot(lhs, half[...], preferred_element_type=jnp.float32)
            if q == 0:
                acc[j, at, :] = value
            else:
                acc[j, at, :] += value
            return 0

        lax.fori_loop(0, size // tile, second, 0)

    def rows_of(c):
        return pl.ds(pl.multiple_of(c * rows, rows), rows)

    def to_sibling(j):
        return remote(sib_out.at[j], sib_in.at[j], b_send.at[j], b_recv.at[j], col=sibling)

    def onward(j, k, way):
        target = (jnp.minimum(z + 1, nz - 1) if way == 0 else jnp.maximum(z - 1, 0)) * 2 + core
        slot = k if way == 0 else jnp.where(k == z - 1, nz, k)
        return remote(z_out.at[j, k], z_in.at[j, slot], z_send.at[j, k], z_recv.at[j, slot], col=target)

    def incoming(j, slot):
        sent = min(slot, nz - 1) if isinstance(slot, int) else slot
        return remote(z_out.at[j, sent], z_in.at[j, slot], z_send.at[j, sent], z_recv.at[j, slot], col=sibling)

    def share(j):
        for k in range(nz):
            sib_out[j, k] = acc[j, rows_of(2 * k + 1 - core), :].astype(jnp.bfloat16)
        to_sibling(j).start()

    def chain(j, action):
        def one_way(way):
            for i in range(nz - 1):
                k = nz - 1 - i if way == 0 else i
                ahead_of = (k > z) if way == 0 else (k < z)
                first = (z == 0) if way == 0 else (z == nz - 1)
                action(j, k, way, ahead_of, first)

        low = z < nz // 2
        pl.when(low)(lambda: one_way(0))
        one_way(1)
        pl.when(jnp.logical_not(low))(lambda: one_way(0))

    def begin(j, k, way, ahead_of, first):
        @pl.when(ahead_of & first)
        def _():
            total = acc[j, rows_of(2 * k + core), :] + sib_in[j, k].astype(jnp.float32)
            z_out[j, k] = total.astype(jnp.bfloat16)
            onward(j, k, way).start()

    def go_on(j, k, way, ahead_of, first):
        @pl.when(ahead_of & jnp.logical_not(first))
        def _():
            total = acc[j, rows_of(2 * k + core), :] + sib_in[j, k].astype(jnp.float32)
            incoming(j, k).wait_recv()
            z_out[j, k] = (total + z_in[j, k].astype(jnp.float32)).astype(jnp.bfloat16)
            onward(j, k, way).start()

    def spread(j):
        to_sibling(j).wait_recv()
        chain(j, begin)

    def finish(j):
        rank = pos * WORK + j
        src = owner_of(rank)
        slot = rank - lookup(start_at, src)
        pair = jnp.clip(lookup([row_at(p) for p in range(n)], src) * slots + slot, 0, n * slots - 1)
        energy = occ[pairs[0, pair]] + occ[pairs[1, pair]]
        here = lax.broadcasted_iota(jnp.int32, (rows, size), 0) + col * rows
        there = lax.broadcasted_iota(jnp.int32, (rows, size), 1)
        levels = jnp.broadcast_to(vir[...], (rows, size))
        mine = jnp.sum(jnp.where(here == there, levels, 0.0), axis=1, keepdims=True)
        denominator = mine + levels - energy
        own = rows_of(col)
        acc[j, own, :] += sib_in[j, z].astype(jnp.float32)

        @pl.when(z > 0)
        def _():
            incoming(j, z).wait_recv()
            acc[j, own, :] += z_in[j, z].astype(jnp.float32)

        @pl.when(z < nz - 1)
        def _():
            incoming(j, nz).wait_recv()
            acc[j, own, :] += z_in[j, nz].astype(jnp.float32)

        ladder = acc[j, own, :]
        t = held[j, col].astype(jnp.float32)
        new = t - (ladder + denominator * t) / (denominator + level_shift)
        ret[reach, j] = new.astype(jnp.bfloat16)
        for d in shifts:
            pl.when(feasible(pos + d, pos, j))(lambda j=j, d=d: give_back(j, d).start())

    for q in range(vectors):
        t = q + ahead + 1
        if q > 0 and t < groups:
            group(t)
        for way in range(2):
            ring(steps - 1, q, way).wait_recv()
        for j in range(WORK):
            if q == 0:
                across(j, 0, 0).wait_recv()
                for h in range(1, nz):
                    for way in range(2):
                        pl.when(arrives(h - 1, way))(lambda j=j, h=h, way=way: across(j, h, way).wait_recv())
            pair_first(q, j)
            if q == vectors - 1 and j > 0:
                spread(j - 1)
            pair_second(q, j)
            if q == vectors - 1:
                share(j)
    for j in range(WORK - 1):
        chain(j, go_on)
    spread(WORK - 1)
    for j in range(WORK - 1):
        finish(j)
    chain(WORK - 1, go_on)
    finish(WORK - 1)
    for j in range(WORK):
        for d in shifts:
            pl.when(feasible(pos, pos + d, j))(lambda j=j, d=d: give_back(j, -d).wait_recv())
    for s in range(slots):
        rank = own_start + s
        where = jnp.clip(rank // WORK - pos + reach, 0, 2 * reach)
        value = ret[where, jnp.clip(rank % WORK, 0, WORK - 1)]
        out[s] = jnp.where(s < own_count, value, jnp.zeros_like(value))

    for j in range(WORK):
        for d in shifts:
            pl.when(feasible(pos, pos + d, j))(lambda j=j, d=d: shuffle(j, d).wait_send())
            pl.when(feasible(pos + d, pos, j))(lambda j=j, d=d: give_back(j, d).wait_send())
        across(j, 0, 0).wait_send()
        for way in range(2):
            for h in range(nz - 1):
                pl.when(leaves(h, way))(lambda j=j, h=h, way=way: along(j, h, way).wait_send())
                pl.when(arrives(h, way))(lambda j=j, h=h, way=way: across(j, h + 1, way).wait_send())
        for k in range(nz):
            pl.when(z != k)(lambda j=j, k=k: incoming(j, k).wait_send())
        to_sibling(j).wait_send()
    for q in range(vectors):
        for step in range(steps):
            for way in range(2):
                ring(step, q, way).wait_send()


def solution(mesh):
    n, m = mesh.shape["row"], mesh.shape["col"]

    def per_device(amplitudes, factors, counts, pair_index, occ_energy, vir_energy):
        slots, rows, size = amplitudes.shape
        vectors, block, _ = factors.shape
        reach = reach_of(n, slots)
        span, nz, steps = 2 * reach + 1, m // 2, n // 2
        bf16, f32 = jnp.bfloat16, jnp.float32
        dma = pltpu.SemaphoreType.DMA
        vmem, smem = pl.BlockSpec(memory_space=pltpu.VMEM), pl.BlockSpec(memory_space=pltpu.SMEM)
        flops = 4 * vectors * WORK * size ** 3
        return pl.pallas_call(
            functools.partial(kernel, n, m, reach),
            out_shape=jax.ShapeDtypeStruct((slots, rows, size), bf16),
            in_specs=[vmem, vmem, smem, smem, smem, vmem],
            out_specs=vmem,
            scratch_shapes=[
                pltpu.VMEM((vectors, n, block, size), bf16),
                pltpu.VMEM((WORK, m, rows, size), bf16),
                pltpu.VMEM((size, size), bf16),
                pltpu.VMEM((WORK, size, size), f32),
                pltpu.VMEM((span, WORK, rows, size), bf16),
                pltpu.VMEM((span, WORK, rows, size), bf16),
                pltpu.VMEM((WORK, nz, rows, size), bf16),
                pltpu.VMEM((WORK, nz, rows, size), bf16),
                pltpu.VMEM((WORK, nz, rows, size), bf16),
                pltpu.VMEM((WORK, nz + 1, rows, size), bf16),
                pltpu.VMEM((span, WORK, rows, size), bf16),
                dma((2, steps, vectors)), dma((2, steps, vectors)),
                dma((span, WORK)), dma((span, WORK)),
                dma((WORK, 2, nz)), dma((WORK, 2, nz)),
                dma((WORK, 2, nz)), dma((WORK, 2, nz)),
                dma((WORK,)), dma((WORK,)),
                dma((WORK, nz)), dma((WORK, nz + 1)),
                dma((span, WORK)), dma((span, WORK)),
            ],
            cost_estimate=pl.CostEstimate(flops=flops, bytes_accessed=2 * vectors * size * size, transcendentals=0),
            compiler_params=pltpu.CompilerParams(
                collective_id=0, has_side_effects=True, vmem_limit_bytes=56 * 2 ** 20),
        )(amplitudes, factors, counts, pair_index.T, occ_energy, vir_energy)

    in_specs = (P("row", "col", None), P("col", "row", None), P(), P(), P(), P())
    return jax.shard_map(
        per_device, mesh=mesh, in_specs=in_specs, out_specs=P("row", "col", None), check_vma=False)
```

```python
import functools

import jax
import jax.numpy as jnp
from jax import lax
from jax.experimental import pallas as pl
from jax.experimental.pallas import tpu as pltpu
from jax.sharding import PartitionSpec as P

WORK = 2
level_shift = 1.0
MESH = pl.DeviceIdType.MESH


def rank_range(pos, n, slots):
    total = WORK * n
    if isinstance(pos, int):
        return max(pos, total - slots * (n - pos)), min(slots * (pos + 1), total - (n - pos - 1))
    low = jnp.maximum(pos, total - slots * (n - pos))
    high = jnp.minimum(slots * (pos + 1), total - (n - pos - 1))
    return low, high


def reach_of(n, slots):
    reach = 0
    for pos in range(n):
        low, high = rank_range(pos, n, slots)
        reach = max([reach] + [abs(k // WORK - pos) for k in range(low, high)])
    return reach


def kernel(n, m, reach, amps, factors, counts, pairs, occ, vir, out,
           full, held, half, acc, stage, shuf, sib_out, sib_in, z_out, z_in, ret,
           l_send, l_recv, s_send, s_recv, t_send, t_recv, f_send, f_recv,
           b_send, b_recv, z_send, z_recv, r_send, r_recv):
    slots, rows, size = amps.shape
    vectors, block = factors.shape[0], factors.shape[1]
    nz = m // 2
    row, col = lax.axis_index("row"), lax.axis_index("col")
    z, core = col // 2, col % 2
    sibling = z * 2 + 1 - core
    pos = row // 2 + (row % 2) * (n - 1 - 2 * (row // 2))

    def row_at(p):
        if isinstance(p, int):
            return 2 * p if p < n // 2 else 2 * (n - 1 - p) + 1
        back = p // (n // 2)
        return (1 - back) * 2 * p + back * (2 * (n - 1 - p) + 1)

    def remote(src, dst, send, recv, **where):
        return pltpu.make_async_remote_copy(
            src_ref=src, dst_ref=dst, send_sem=send, recv_sem=recv, device_id=where, device_id_type=MESH)

    barrier = pltpu.get_barrier_semaphore()
    for step in range(1, n):
        pl.semaphore_signal(barrier, inc=1, device_id={"row": (row + step) % n}, device_id_type=MESH)
    for step in range(1, m):
        pl.semaphore_signal(barrier, inc=1, device_id={"col": (col + step) % m}, device_id_type=MESH)

    count_at = [counts[row_at(p)] for p in range(n)]
    start_at, running = [], jnp.int32(0)
    for p in range(n):
        start_at.append(running)
        running = running + count_at[p]

    def lookup(values, p):
        found = jnp.int32(0)
        for i in range(n):
            found = jnp.where(p == i, values[i], found)
        return found

    own_start, own_count = lookup(start_at, pos), lookup(count_at, pos)

    def owner_of(rank):
        src = jnp.int32(0)
        for p in range(n - 1):
            src = src + jnp.where(start_at[p] + count_at[p] <= rank, 1, 0)
        return src

    def feasible(p, worker, j):
        low, high = rank_range(p, n, slots)
        rank = worker * WORK + j
        return (p >= 0) & (p < n) & (worker >= 0) & (worker < n) & (rank >= low) & (rank < high)

    shifts = [d for d in range(-reach, reach + 1) if d != 0]
    for j in range(WORK):
        for d in shifts:
            slot = jnp.clip((pos + d) * WORK + j - own_start, 0, slots - 1)
            stage[d + reach, j] = amps[slot]
        shuf[reach, j] = amps[jnp.clip(pos * WORK + j - own_start, 0, slots - 1)]

    pl.semaphore_wait(barrier, n + m - 2)

    def shuffle(j, d):
        target = row_at((pos + d + n) % n)
        return remote(stage.at[d + reach, j], shuf.at[reach - d, j], s_send.at[d + reach, j], s_recv.at[reach - d, j],
                      row=target)

    def give_back(j, d):
        target = row_at((pos + d + n) % n)
        return remote(ret.at[reach, j], ret.at[reach - d, j], r_send.at[d + reach, j], r_recv.at[reach - d, j],
                      row=target)

    for j in range(WORK):
        for d in shifts:
            pl.when(feasible(pos, pos + d, j))(lambda j=j, d=d: shuffle(j, d).start())

    steps = n // 2
    part = block // 2
    lead = 3

    def ring(step, q, way):
        move = 1 if way == 0 else -1
        origin = row_at((pos - move * step + n) % n)
        target = row_at((pos + move + n) % n)
        src = factors.at[q] if step == 0 else full.at[q, origin]
        dst = full.at[q, origin]
        if step == steps - 1:
            cut = pl.ds(way * part, part)
            src, dst = src.at[cut], dst.at[cut]
        return remote(src, dst, l_send.at[way, step, q], l_recv.at[way, step, q], row=target)

    def group(t):
        for step in range(steps - 1, -1, -1):
            q = t - lead * step
            if 0 <= q < vectors:
                for way in range(2):
                    if step > 0:
                        ring(step - 1, q, way).wait_recv()
                    ring(step, q, way).start()

    groups = vectors + lead * (steps - 1)
    ahead = lead * (steps - 1)
    for t in range(min(lead, groups)):
        group(t)

    def own_block(q, _):
        full[q, row] = factors[q]
        return 0

    lax.fori_loop(0, vectors, own_block, 0)

    def passed(h, way):
        return z - h if way == 0 else z + h

    def arrives(h, way):
        return passed(h + 1, way) >= 0 if way == 0 else passed(h + 1, way) < nz

    def leaves(h, way):
        there = passed(h, way) >= 0 if way == 0 else passed(h, way) < nz
        return there & (z + 1 < nz if way == 0 else z > 0)

    def along(j, h, way):
        src = passed(h, way) * 2 + core
        target = (jnp.minimum(z + 1, nz - 1) if way == 0 else jnp.maximum(z - 1, 0)) * 2 + core
        return remote(held.at[j, src], held.at[j, src], t_send.at[j, way, h], t_recv.at[j, way, h], col=target)

    def across(j, h, way):
        src = passed(h, way) * 2 + core
        return remote(held.at[j, src], held.at[j, src], f_send.at[j, way, h], f_recv.at[j, way, h], col=sibling)

    def hop(j, h, way):
        @pl.when(arrives(h - 1, way))
        def _():
            along(j, h - 1, way).wait_recv()
            if h < nz - 1:
                pl.when(leaves(h, way))(lambda: along(j, h, way).start())
            across(j, h, way).start()

    for j in range(WORK):
        for d in shifts:
            pl.when(feasible(pos - d, pos, j))(lambda j=j, d=d: shuffle(j, d).wait_recv())
        src = owner_of(pos * WORK + j) - pos
        chosen = shuf[reach, j]
        for d in shifts:
            chosen = jnp.where(src == d, shuf[d + reach, j], chosen)
        held[j, col] = chosen
        for way in range(2):
            pl.when(leaves(0, way))(lambda j=j, way=way: along(j, 0, way).start())
        across(j, 0, 0).start()

    later = list(range(lead, min(ahead + 2, groups)))
    for h in range(1, nz):
        for j in range(WORK):
            for way in range(2):
                hop(j, h, way)
        if later and h > 1:
            group(later.pop(0))
    for t in later:
        group(t)

    tile = 256 if size % 256 == 0 else size

    def both_first(q):
        def first(i, _):
            at = pl.ds(pl.multiple_of(i * tile, tile), tile)
            lhs = held[...].reshape(WORK * size, size)
            rhs = full.at[q].reshape(size, size)[at, :]
            half[:, at] = lax.dot_general(
                lhs, rhs, (((1,), (1,)), ((), ())), preferred_element_type=jnp.float32).astype(jnp.bfloat16)
            return 0

        lax.fori_loop(0, size // tile, first, 0)

    def pair_second(q, j, low, high):
        def second(i, _):
            at = pl.ds(pl.multiple_of(i * tile, tile), tile)
            lhs = full[q].reshape(size, size)
            value = jnp.dot(lhs, half[pl.ds(j * size, size), at], preferred_element_type=jnp.float32)
            if q == 0:
                acc[j, :, at] = value
            else:
                acc[j, :, at] += value
            return 0

        lax.fori_loop(low, high, second, 0)

    def rows_of(c):
        return pl.ds(pl.multiple_of(c * rows, rows), rows)

    def to_sibling(j):
        return remote(sib_out.at[j], sib_in.at[j], b_send.at[j], b_recv.at[j], col=sibling)

    def onward(j, k, way):
        target = (jnp.minimum(z + 1, nz - 1) if way == 0 else jnp.maximum(z - 1, 0)) * 2 + core
        slot = k if way == 0 else jnp.where(k == z - 1, nz, k)
        return remote(z_out.at[j, k], z_in.at[j, slot], z_send.at[j, k], z_recv.at[j, slot], col=target)

    def incoming(j, slot):
        sent = min(slot, nz - 1) if isinstance(slot, int) else slot
        return remote(z_out.at[j, sent], z_in.at[j, slot], z_send.at[j, sent], z_recv.at[j, slot], col=sibling)

    def share(j):
        for k in range(nz):
            sib_out[j, k] = acc[j, rows_of(2 * k + 1 - core), :].astype(jnp.bfloat16)
        to_sibling(j).start()

    def chain(j, action):
        def one_way(way):
            for i in range(nz - 1):
                k = nz - 1 - i if way == 0 else i
                ahead_of = (k > z) if way == 0 else (k < z)
                first = (z == 0) if way == 0 else (z == nz - 1)
                action(j, k, way, ahead_of, first)

        low = z < nz // 2
        pl.when(low)(lambda: one_way(0))
        one_way(1)
        pl.when(jnp.logical_not(low))(lambda: one_way(0))

    def begin(j, k, way, ahead_of, first):
        @pl.when(ahead_of & first)
        def _():
            total = acc[j, rows_of(2 * k + core), :] + sib_in[j, k].astype(jnp.float32)
            z_out[j, k] = total.astype(jnp.bfloat16)
            onward(j, k, way).start()

    def go_on(j, k, way, ahead_of, first):
        @pl.when(ahead_of & jnp.logical_not(first))
        def _():
            total = acc[j, rows_of(2 * k + core), :] + sib_in[j, k].astype(jnp.float32)
            incoming(j, k).wait_recv()
            z_out[j, k] = (total + z_in[j, k].astype(jnp.float32)).astype(jnp.bfloat16)
            onward(j, k, way).start()

    def spread(j):
        to_sibling(j).wait_recv()
        chain(j, begin)

    def finish(j):
        rank = pos * WORK + j
        src = owner_of(rank)
        slot = rank - lookup(start_at, src)
        pair = jnp.clip(lookup([row_at(p) for p in range(n)], src) * slots + slot, 0, n * slots - 1)
        energy = occ[pairs[0, pair]] + occ[pairs[1, pair]]
        here = lax.broadcasted_iota(jnp.int32, (rows, size), 0) + col * rows
        there = lax.broadcasted_iota(jnp.int32, (rows, size), 1)
        levels = jnp.broadcast_to(vir[...], (rows, size))
        mine = jnp.sum(jnp.where(here == there, levels, 0.0), axis=1, keepdims=True)
        denominator = mine + levels - energy
        own = rows_of(col)
        acc[j, own, :] += sib_in[j, z].astype(jnp.float32)

        @pl.when(z > 0)
        def _():
            incoming(j, z).wait_recv()
            acc[j, own, :] += z_in[j, z].astype(jnp.float32)

        @pl.when(z < nz - 1)
        def _():
            incoming(j, nz).wait_recv()
            acc[j, own, :] += z_in[j, nz].astype(jnp.float32)

        ladder = acc[j, own, :]
        t = held[j, col].astype(jnp.float32)
        new = t - (ladder + denominator * t) / (denominator + level_shift)
        ret[reach, j] = new.astype(jnp.bfloat16)
        for d in shifts:
            pl.when(feasible(pos + d, pos, j))(lambda j=j, d=d: give_back(j, d).start())

    for q in range(vectors):
        t = q + ahead + 1
        if q > 0 and t < groups:
            group(t)
        for way in range(2):
            ring(steps - 1, q, way).wait_recv()
        if q == 0:
            for j in range(WORK):
                across(j, 0, 0).wait_recv()
                for h in range(1, nz):
                    for way in range(2):
                        pl.when(arrives(h - 1, way))(lambda j=j, h=h, way=way: across(j, h, way).wait_recv())
        both_first(q)
        for j in range(WORK):
            tiles = size // tile
            if q == vectors - 1 and j > 0:
                pair_second(q, j, 0, tiles // 2)
                spread(j - 1)
                pair_second(q, j, tiles // 2, tiles)
            else:
                pair_second(q, j, 0, tiles)
            if q == vectors - 1:
                share(j)
    for j in range(WORK - 1):
        chain(j, go_on)
    spread(WORK - 1)
    for j in range(WORK - 1):
        finish(j)
    chain(WORK - 1, go_on)
    finish(WORK - 1)
    for j in range(WORK):
        for d in shifts:
            pl.when(feasible(pos, pos + d, j))(lambda j=j, d=d: give_back(j, -d).wait_recv())
    for s in range(slots):
        rank = own_start + s
        where = jnp.clip(rank // WORK - pos + reach, 0, 2 * reach)
        value = ret[where, jnp.clip(rank % WORK, 0, WORK - 1)]
        out[s] = jnp.where(s < own_count, value, jnp.zeros_like(value))

    for j in range(WORK):
        for d in shifts:
            pl.when(feasible(pos, pos + d, j))(lambda j=j, d=d: shuffle(j, d).wait_send())
            pl.when(feasible(pos + d, pos, j))(lambda j=j, d=d: give_back(j, d).wait_send())
        across(j, 0, 0).wait_send()
        for way in range(2):
            for h in range(nz - 1):
                pl.when(leaves(h, way))(lambda j=j, h=h, way=way: along(j, h, way).wait_send())
                pl.when(arrives(h, way))(lambda j=j, h=h, way=way: across(j, h + 1, way).wait_send())
        for k in range(nz):
            pl.when(z != k)(lambda j=j, k=k: incoming(j, k).wait_send())
        to_sibling(j).wait_send()
    for q in range(vectors):
        for step in range(steps):
            for way in range(2):
                ring(step, q, way).wait_send()


def solution(mesh):
    n, m = mesh.shape["row"], mesh.shape["col"]

    def per_device(amplitudes, factors, counts, pair_index, occ_energy, vir_energy):
        slots, rows, size = amplitudes.shape
        vectors, block, _ = factors.shape
        reach = reach_of(n, slots)
        span, nz, steps = 2 * reach + 1, m // 2, n // 2
        bf16, f32 = jnp.bfloat16, jnp.float32
        dma = pltpu.SemaphoreType.DMA
        vmem, smem = pl.BlockSpec(memory_space=pltpu.VMEM), pl.BlockSpec(memory_space=pltpu.SMEM)
        flops = 4 * vectors * WORK * size ** 3
        return pl.pallas_call(
            functools.partial(kernel, n, m, reach),
            out_shape=jax.ShapeDtypeStruct((slots, rows, size), bf16),
            in_specs=[vmem, vmem, smem, smem, smem, vmem],
            out_specs=vmem,
            scratch_shapes=[
                pltpu.VMEM((vectors, n, block, size), bf16),
                pltpu.VMEM((WORK, m, rows, size), bf16),
                pltpu.VMEM((WORK * size, size), bf16),
                pltpu.VMEM((WORK, size, size), f32),
                pltpu.VMEM((span, WORK, rows, size), bf16),
                pltpu.VMEM((span, WORK, rows, size), bf16),
                pltpu.VMEM((WORK, nz, rows, size), bf16),
                pltpu.VMEM((WORK, nz, rows, size), bf16),
                pltpu.VMEM((WORK, nz, rows, size), bf16),
                pltpu.VMEM((WORK, nz + 1, rows, size), bf16),
                pltpu.VMEM((span, WORK, rows, size), bf16),
                dma((2, steps, vectors)), dma((2, steps, vectors)),
                dma((span, WORK)), dma((span, WORK)),
                dma((WORK, 2, nz)), dma((WORK, 2, nz)),
                dma((WORK, 2, nz)), dma((WORK, 2, nz)),
                dma((WORK,)), dma((WORK,)),
                dma((WORK, nz)), dma((WORK, nz + 1)),
                dma((span, WORK)), dma((span, WORK)),
            ],
            cost_estimate=pl.CostEstimate(flops=flops, bytes_accessed=2 * vectors * size * size, transcendentals=0),
            compiler_params=pltpu.CompilerParams(
                collective_id=0, has_side_effects=True, vmem_limit_bytes=56 * 2 ** 20),
        )(amplitudes, factors, counts, pair_index.T, occ_energy, vir_energy)

    in_specs = (P("row", "col", None), P("col", "row", None), P(), P(), P(), P())
    return jax.shard_map(
        per_device, mesh=mesh, in_specs=in_specs, out_specs=P("row", "col", None), check_vma=False)
```

```python
import functools

import jax
import jax.numpy as jnp
from jax import lax
from jax.experimental import pallas as pl
from jax.experimental.pallas import tpu as pltpu
from jax.sharding import PartitionSpec as P

WORK = 2
level_shift = 1.0
MESH = pl.DeviceIdType.MESH


def rank_range(pos, n, slots):
    total = WORK * n
    if isinstance(pos, int):
        return max(pos, total - slots * (n - pos)), min(slots * (pos + 1), total - (n - pos - 1))
    low = jnp.maximum(pos, total - slots * (n - pos))
    high = jnp.minimum(slots * (pos + 1), total - (n - pos - 1))
    return low, high


def reach_of(n, slots):
    reach = 0
    for pos in range(n):
        low, high = rank_range(pos, n, slots)
        reach = max([reach] + [abs(k // WORK - pos) for k in range(low, high)])
    return reach


def kernel(n, m, reach, amps, factors, counts, pairs, occ, vir, out,
           full, held, half, half_far, acc_s, acc_b, stage, shuf, sib_out_s, sib_out_b, sib_in_s, sib_in_b,
           z_out_s, z_out_b, z_in_s, z_in_b, lad, ret,
           l_send, l_recv, s_send, s_recv, t_send, t_recv, f_send, f_recv,
           b_send, b_recv, z_send, z_recv, r_send, r_recv):
    acc, sib_out, sib_in = (acc_s, acc_b), (sib_out_s, sib_out_b), (sib_in_s, sib_in_b)
    z_out, z_in = (z_out_s, z_out_b), (z_in_s, z_in_b)
    slots, rows, size = amps.shape
    vectors, block = factors.shape[0], factors.shape[1]
    nz = m // 2
    row, col = lax.axis_index("row"), lax.axis_index("col")
    z, core = col // 2, col % 2
    sibling = z * 2 + 1 - core
    pos = row // 2 + (row % 2) * (n - 1 - 2 * (row // 2))

    def row_at(p):
        if isinstance(p, int):
            return 2 * p if p < n // 2 else 2 * (n - 1 - p) + 1
        back = p // (n // 2)
        return (1 - back) * 2 * p + back * (2 * (n - 1 - p) + 1)

    def remote(src, dst, send, recv, **where):
        return pltpu.make_async_remote_copy(
            src_ref=src, dst_ref=dst, send_sem=send, recv_sem=recv, device_id=where, device_id_type=MESH)

    barrier = pltpu.get_barrier_semaphore()
    for step in range(1, n):
        pl.semaphore_signal(barrier, inc=1, device_id={"row": (row + step) % n}, device_id_type=MESH)
    for step in range(1, m):
        pl.semaphore_signal(barrier, inc=1, device_id={"col": (col + step) % m}, device_id_type=MESH)

    count_at = [counts[row_at(p)] for p in range(n)]
    start_at, running = [], jnp.int32(0)
    for p in range(n):
        start_at.append(running)
        running = running + count_at[p]

    def lookup(values, p):
        found = jnp.int32(0)
        for i in range(n):
            found = jnp.where(p == i, values[i], found)
        return found

    own_start, own_count = lookup(start_at, pos), lookup(count_at, pos)

    def owner_of(rank):
        src = jnp.int32(0)
        for p in range(n - 1):
            src = src + jnp.where(start_at[p] + count_at[p] <= rank, 1, 0)
        return src

    def feasible(p, worker, j):
        low, high = rank_range(p, n, slots)
        rank = worker * WORK + j
        return (p >= 0) & (p < n) & (worker >= 0) & (worker < n) & (rank >= low) & (rank < high)

    shifts = [d for d in range(-reach, reach + 1) if d != 0]
    for j in range(WORK):
        for d in shifts:
            slot = jnp.clip((pos + d) * WORK + j - own_start, 0, slots - 1)
            stage[d + reach, j] = amps[slot]
        shuf[reach, j] = amps[jnp.clip(pos * WORK + j - own_start, 0, slots - 1)]

    pl.semaphore_wait(barrier, n + m - 2)

    def shuffle(j, d):
        target = row_at((pos + d + n) % n)
        return remote(stage.at[d + reach, j], shuf.at[reach - d, j], s_send.at[d + reach, j], s_recv.at[reach - d, j],
                      row=target)

    def give_back(j, d):
        target = row_at((pos + d + n) % n)
        return remote(ret.at[reach, j], ret.at[reach - d, j], r_send.at[d + reach, j], r_recv.at[reach - d, j],
                      row=target)

    for j in range(WORK):
        for d in shifts:
            pl.when(feasible(pos, pos + d, j))(lambda j=j, d=d: shuffle(j, d).start())

    steps = n // 2
    part = block // 2
    lead = vectors

    def place(step, way):
        return 0 if step == 0 else (n - 1 if step == steps else 2 * step - 1 + way)

    def ring(step, q, way):
        target = row_at((pos + (1 if way == 0 else -1) + n) % n)
        src = factors.at[q] if step == 0 else full.at[q, place(step, way)]
        dst = full.at[q, place(step + 1, way)]
        if step == steps - 1:
            cut = pl.ds(way * part, part)
            src, dst = src.at[cut], dst.at[cut]
        return remote(src, dst, l_send.at[way, step, q], l_recv.at[way, step, q], row=target)

    def group(t):
        for step in range(steps - 1, -1, -1):
            q = t - lead * step
            if 0 <= q < vectors:
                for way in range(2):
                    if step > 0:
                        ring(step - 1, q, way).wait_recv()
                    ring(step, q, way).start()

    for t in range(lead * (steps - 1)):
        group(t)

    def own_block(q, _):
        full[q, 0] = factors[q]
        return 0

    lax.fori_loop(0, vectors, own_block, 0)

    def passed(h, way):
        return z - h if way == 0 else z + h

    def arrives(h, way):
        return passed(h + 1, way) >= 0 if way == 0 else passed(h + 1, way) < nz

    def leaves(h, way):
        there = passed(h, way) >= 0 if way == 0 else passed(h, way) < nz
        return there & (z + 1 < nz if way == 0 else z > 0)

    def along(j, h, way):
        src = passed(h, way) * 2 + core
        target = (jnp.minimum(z + 1, nz - 1) if way == 0 else jnp.maximum(z - 1, 0)) * 2 + core
        return remote(held.at[j, src], held.at[j, src], t_send.at[j, way, h], t_recv.at[j, way, h], col=target)

    def across(j, h, way):
        src = passed(h, way) * 2 + core
        return remote(held.at[j, src], held.at[j, src], f_send.at[j, way, h], f_recv.at[j, way, h], col=sibling)

    def hop(j, h, way):
        @pl.when(arrives(h - 1, way))
        def _():
            along(j, h - 1, way).wait_recv()
            if h < nz - 1:
                pl.when(leaves(h, way))(lambda: along(j, h, way).start())
            across(j, h, way).start()

    for j in range(WORK):
        for d in shifts:
            pl.when(feasible(pos - d, pos, j))(lambda j=j, d=d: shuffle(j, d).wait_recv())
        src = owner_of(pos * WORK + j) - pos
        chosen = shuf[reach, j]
        for d in shifts:
            chosen = jnp.where(src == d, shuf[d + reach, j], chosen)
        held[j, col] = chosen
        for way in range(2):
            pl.when(leaves(0, way))(lambda j=j, way=way: along(j, 0, way).start())
        across(j, 0, 0).start()

    for h in range(1, nz):
        for j in range(WORK):
            for way in range(2):
                hop(j, h, way)

    near = (n - 1) * block

    def dot_t(x, y):
        return lax.dot_general(x, y, (((1,), (1,)), ((), ())), preferred_element_type=jnp.float32)

    def near_first(q):
        def one(j, _):
            value = dot_t(held[j].reshape(size, size), full[q, 0:n - 1].reshape(near, size))
            half[q, j] = value.astype(jnp.bfloat16)
            return 0

        lax.fori_loop(0, WORK, one, 0)

    def near_second(q, j):
        value = jnp.dot(full[q, 0:n - 1].reshape(near, size), half[q, j], preferred_element_type=jnp.float32)
        if q == 0:
            acc_s[j, 0:near, :] = value
        else:
            acc_s[j, 0:near, :] += value

    def far(q, j):
        value = dot_t(held[j].reshape(size, size), full[q, n - 1])
        half_far[...] = value.astype(jnp.bfloat16)
        value = jnp.dot(full[q].reshape(size, size), half_far[...], preferred_element_type=jnp.float32)
        corner = jnp.dot(full[q, n - 1], half[q, j], preferred_element_type=jnp.float32)
        if q == 0:
            acc_b[j] = value
            acc_s[j, near:size, :] = corner
        else:
            acc_b[j] += value
            acc_s[j, near:size, :] += corner

    def place_of(b):
        p = b // 2 + (b % 2) * (n - 1 - 2 * (b // 2))
        d = (p - pos + n) % n
        return jnp.where(d == n // 2, n - 1, jnp.where(d < n // 2, 2 * d, 2 * (n - d) - 1))

    def is_far(c):
        return place_of((c * rows) // block) == n - 1

    def rows_of(c):
        start = place_of((c * rows) // block) * block + (c * rows) % block
        return pl.ds(pl.multiple_of(start, rows), rows)

    def ready(stage_of, c):
        if stage_of == 2:
            return c >= 0
        return is_far(c) if stage_of == 1 else jnp.logical_not(is_far(c))

    def to_sibling(w, j, k):
        return remote(sib_out[w].at[j, k], sib_in[w].at[j, k], b_send.at[w, j, k], b_recv.at[w, j, k], col=sibling)

    def onward(w, j, k, way):
        target = (jnp.minimum(z + 1, nz - 1) if way == 0 else jnp.maximum(z - 1, 0)) * 2 + core
        slot = k if way == 0 else jnp.where(k == z - 1, nz, k)
        return remote(z_out[w].at[j, k], z_in[w].at[j, slot], z_send.at[w, j, k], z_recv.at[w, j, slot], col=target)

    def incoming(w, j, slot):
        sent = min(slot, nz - 1) if isinstance(slot, int) else slot
        return remote(z_out[w].at[j, sent], z_in[w].at[j, slot], z_send.at[w, j, sent], z_recv.at[w, j, slot],
                      col=sibling)

    def share(stage_of, j):
        w = stage_of // 2
        for k in range(nz):
            c = 2 * k + 1 - core

            @pl.when(ready(stage_of, c))
            def _():
                sib_out[w][j, k] = acc[w][j, rows_of(c), :].astype(jnp.bfloat16)
                to_sibling(w, j, k).start()

    def chain(stage_of, j, begins):
        w = stage_of // 2

        def one_way(way):
            for i in range(nz - 1):
                k = nz - 1 - i if way == 0 else i
                c = 2 * k + core
                first = (z == 0) if way == 0 else (z == nz - 1)
                first = first if begins else jnp.logical_not(first)

                @pl.when(((k > z) if way == 0 else (k < z)) & first & ready(stage_of, c))
                def _():
                    to_sibling(w, j, k).wait_recv()
                    total = acc[w][j, rows_of(c), :] + sib_in[w][j, k].astype(jnp.float32)
                    if not begins:
                        incoming(w, j, k).wait_recv()
                        total = total + z_in[w][j, k].astype(jnp.float32)
                    z_out[w][j, k] = total.astype(jnp.bfloat16)
                    onward(w, j, k, way).start()

        if begins:
            one_way(0)
            one_way(1)
        else:
            low = z < nz // 2
            pl.when(low)(lambda: one_way(0))
            one_way(1)
            pl.when(jnp.logical_not(low))(lambda: one_way(0))

    def finish(j):
        rank = pos * WORK + j
        src = owner_of(rank)
        slot = rank - lookup(start_at, src)
        pair = jnp.clip(lookup([row_at(p) for p in range(n)], src) * slots + slot, 0, n * slots - 1)
        energy = occ[pairs[0, pair]] + occ[pairs[1, pair]]
        here = lax.broadcasted_iota(jnp.int32, (rows, size), 0) + col * rows
        there = lax.broadcasted_iota(jnp.int32, (rows, size), 1)
        levels = jnp.broadcast_to(vir[...], (rows, size))
        mine = jnp.sum(jnp.where(here == there, levels, 0.0), axis=1, keepdims=True)
        denominator = mine + levels - energy
        own = rows_of(col)
        for w in range(2):
            to_sibling(w, j, z).wait_recv()
            acc[w][j, own, :] += sib_in[w][j, z].astype(jnp.float32)

        @pl.when(z > 0)
        def _():
            for w in range(2):
                incoming(w, j, z).wait_recv()
                acc[w][j, own, :] += z_in[w][j, z].astype(jnp.float32)

        @pl.when(z < nz - 1)
        def _():
            for w in range(2):
                incoming(w, j, nz).wait_recv()
                acc[w][j, own, :] += z_in[w][j, nz].astype(jnp.float32)

        for b in range(n):
            for i in range(n):
                @pl.when(place_of(b) == i)
                def _(b=b, i=i):
                    if i < n - 1:
                        piece = acc_s[j, own, i * block:(i + 1) * block]
                    else:
                        piece = acc_b[j, own, :]
                    lad[:, b * block:(b + 1) * block] = piece
        ladder = lad[...]
        t = held[j, col].astype(jnp.float32)
        new = t - (ladder + denominator * t) / (denominator + level_shift)
        ret[reach, j] = new.astype(jnp.bfloat16)
        for d in shifts:
            pl.when(feasible(pos + d, pos, j))(lambda j=j, d=d: give_back(j, d).start())

    last = vectors - 1
    for j in range(WORK):
        across(j, 0, 0).wait_recv()
        for h in range(1, nz):
            for way in range(2):
                pl.when(arrives(h - 1, way))(lambda j=j, h=h, way=way: across(j, h, way).wait_recv())
    sent = 0
    for q in range(vectors):
        while sent < min(vectors, q + 3):
            group(lead * (steps - 1) + sent)
            sent += 1
        near_first(q)
        for j in range(WORK):
            near_second(q, j)
            if q == last:
                share(0, j)
    for q in range(vectors):
        for way in range(2):
            ring(steps - 1, q, way).wait_recv()
        for j in range(WORK):
            far(q, j)
            if q == last:
                share(1, j)
                share(2, j)
        if q == 0:
            for j in range(WORK):
                chain(0, j, True)
        elif q == 1:
            chain(0, 0, False)
        elif q == 2:
            chain(0, 1, False)
    for j in range(WORK):
        for kind in (1, 2):
            chain(kind, j, True)
    for j in range(WORK):
        for kind in (1, 2):
            chain(kind, j, False)
        finish(j)
    for j in range(WORK):
        for d in shifts:
            pl.when(feasible(pos, pos + d, j))(lambda j=j, d=d: give_back(j, -d).wait_recv())
    for s in range(slots):
        rank = own_start + s
        where = jnp.clip(rank // WORK - pos + reach, 0, 2 * reach)
        value = ret[where, jnp.clip(rank % WORK, 0, WORK - 1)]
        out[s] = jnp.where(s < own_count, value, jnp.zeros_like(value))

    for j in range(WORK):
        for d in shifts:
            pl.when(feasible(pos, pos + d, j))(lambda j=j, d=d: shuffle(j, d).wait_send())
            pl.when(feasible(pos + d, pos, j))(lambda j=j, d=d: give_back(j, d).wait_send())
        across(j, 0, 0).wait_send()
        for way in range(2):
            for h in range(nz - 1):
                pl.when(leaves(h, way))(lambda j=j, h=h, way=way: along(j, h, way).wait_send())
                pl.when(arrives(h, way))(lambda j=j, h=h, way=way: across(j, h + 1, way).wait_send())
        for k in range(nz):
            for w in range(2):
                pl.when(z != k)(lambda j=j, k=k, w=w: incoming(w, j, k).wait_send())
                to_sibling(w, j, k).wait_send()
    for q in range(vectors):
        for step in range(steps):
            for way in range(2):
                ring(step, q, way).wait_send()


def solution(mesh):
    n, m = mesh.shape["row"], mesh.shape["col"]

    def per_device(amplitudes, factors, counts, pair_index, occ_energy, vir_energy):
        slots, rows, size = amplitudes.shape
        vectors, block, _ = factors.shape
        reach = reach_of(n, slots)
        span, nz, steps = 2 * reach + 1, m // 2, n // 2
        near = (n - 1) * block
        bf16, f32 = jnp.bfloat16, jnp.float32
        dma = pltpu.SemaphoreType.DMA
        vmem, smem = pl.BlockSpec(memory_space=pltpu.VMEM), pl.BlockSpec(memory_space=pltpu.SMEM)
        flops = 4 * vectors * WORK * size ** 3
        return pl.pallas_call(
            functools.partial(kernel, n, m, reach),
            out_shape=jax.ShapeDtypeStruct((slots, rows, size), bf16),
            in_specs=[vmem, vmem, smem, smem, smem, vmem],
            out_specs=vmem,
            scratch_shapes=[
                pltpu.VMEM((vectors, n, block, size), bf16),
                pltpu.VMEM((WORK, m, rows, size), bf16),
                pltpu.VMEM((vectors, WORK, size, near), bf16),
                pltpu.VMEM((size, block), bf16),
                pltpu.VMEM((WORK, size, near), f32),
                pltpu.VMEM((WORK, size, block), f32),
                pltpu.VMEM((span, WORK, rows, size), bf16),
                pltpu.VMEM((span, WORK, rows, size), bf16),
                pltpu.VMEM((WORK, nz, rows, near), bf16),
                pltpu.VMEM((WORK, nz, rows, block), bf16),
                pltpu.VMEM((WORK, nz, rows, near), bf16),
                pltpu.VMEM((WORK, nz, rows, block), bf16),
                pltpu.VMEM((WORK, nz, rows, near), bf16),
                pltpu.VMEM((WORK, nz, rows, block), bf16),
                pltpu.VMEM((WORK, nz + 1, rows, near), bf16),
                pltpu.VMEM((WORK, nz + 1, rows, block), bf16),
                pltpu.VMEM((rows, size), f32),
                pltpu.VMEM((span, WORK, rows, size), bf16),
                dma((2, steps, vectors)), dma((2, steps, vectors)),
                dma((span, WORK)), dma((span, WORK)),
                dma((WORK, 2, nz)), dma((WORK, 2, nz)),
                dma((WORK, 2, nz)), dma((WORK, 2, nz)),
                dma((2, WORK, nz)), dma((2, WORK, nz)),
                dma((2, WORK, nz)), dma((2, WORK, nz + 1)),
                dma((span, WORK)), dma((span, WORK)),
            ],
            cost_estimate=pl.CostEstimate(flops=flops, bytes_accessed=2 * vectors * size * size, transcendentals=0),
            compiler_params=pltpu.CompilerParams(
                collective_id=0, has_side_effects=True, vmem_limit_bytes=56 * 2 ** 20),
        )(amplitudes, factors, counts, pair_index.T, occ_energy, vir_energy)

    in_specs = (P("row", "col", None), P("col", "row", None), P(), P(), P(), P())
    return jax.shard_map(
        per_device, mesh=mesh, in_specs=in_specs, out_specs=P("row", "col", None), check_vma=False)
```

```python
import functools

import jax
import jax.numpy as jnp
from jax import lax
from jax.experimental import pallas as pl
from jax.experimental.pallas import tpu as pltpu
from jax.sharding import PartitionSpec as P

WORK = 2
level_shift = 1.0
MESH = pl.DeviceIdType.MESH


def rank_range(pos, n, slots):
    total = WORK * n
    if isinstance(pos, int):
        return max(pos, total - slots * (n - pos)), min(slots * (pos + 1), total - (n - pos - 1))
    low = jnp.maximum(pos, total - slots * (n - pos))
    high = jnp.minimum(slots * (pos + 1), total - (n - pos - 1))
    return low, high


def reach_of(n, slots):
    reach = 0
    for pos in range(n):
        low, high = rank_range(pos, n, slots)
        reach = max([reach] + [abs(k // WORK - pos) for k in range(low, high)])
    return reach


def kernel(n, m, reach, amps, factors, counts, pairs, occ, vir, out,
           full, held, half, acc, stage, shuf, sib_out, sib_in, z_out, z_in, ret,
           l_send, l_recv, s_send, s_recv, t_send, t_recv, f_send, f_recv,
           b_send, b_recv, z_send, z_recv, r_send, r_recv):
    slots, rows, size = amps.shape
    vectors, block = factors.shape[0], factors.shape[1]
    nz = m // 2
    row, col = lax.axis_index("row"), lax.axis_index("col")
    z, core = col // 2, col % 2
    sibling = z * 2 + 1 - core
    pos = row // 2 + (row % 2) * (n - 1 - 2 * (row // 2))

    def row_at(p):
        if isinstance(p, int):
            return 2 * p if p < n // 2 else 2 * (n - 1 - p) + 1
        back = p // (n // 2)
        return (1 - back) * 2 * p + back * (2 * (n - 1 - p) + 1)

    def remote(src, dst, send, recv, **where):
        return pltpu.make_async_remote_copy(
            src_ref=src, dst_ref=dst, send_sem=send, recv_sem=recv, device_id=where, device_id_type=MESH)

    barrier = pltpu.get_barrier_semaphore()
    for step in range(1, n):
        pl.semaphore_signal(barrier, inc=1, device_id={"row": (row + step) % n}, device_id_type=MESH)
    for step in range(1, m):
        pl.semaphore_signal(barrier, inc=1, device_id={"col": (col + step) % m}, device_id_type=MESH)

    count_at = [counts[row_at(p)] for p in range(n)]
    start_at, running = [], jnp.int32(0)
    for p in range(n):
        start_at.append(running)
        running = running + count_at[p]

    def lookup(values, p):
        found = jnp.int32(0)
        for i in range(n):
            found = jnp.where(p == i, values[i], found)
        return found

    own_start, own_count = lookup(start_at, pos), lookup(count_at, pos)

    def owner_of(rank):
        src = jnp.int32(0)
        for p in range(n - 1):
            src = src + jnp.where(start_at[p] + count_at[p] <= rank, 1, 0)
        return src

    def feasible(p, worker, j):
        low, high = rank_range(p, n, slots)
        rank = worker * WORK + j
        return (p >= 0) & (p < n) & (worker >= 0) & (worker < n) & (rank >= low) & (rank < high)

    shifts = [d for d in range(-reach, reach + 1) if d != 0]
    for j in range(WORK):
        for d in shifts:
            slot = jnp.clip((pos + d) * WORK + j - own_start, 0, slots - 1)
            stage[d + reach, j] = amps[slot]
        shuf[reach, j] = amps[jnp.clip(pos * WORK + j - own_start, 0, slots - 1)]

    pl.semaphore_wait(barrier, n + m - 2)

    def shuffle(j, d):
        target = row_at((pos + d + n) % n)
        return remote(stage.at[d + reach, j], shuf.at[reach - d, j], s_send.at[d + reach, j], s_recv.at[reach - d, j],
                      row=target)

    def give_back(j, d):
        target = row_at((pos + d + n) % n)
        return remote(ret.at[reach, j], ret.at[reach - d, j], r_send.at[d + reach, j], r_recv.at[reach - d, j],
                      row=target)

    for j in range(WORK):
        for d in shifts:
            pl.when(feasible(pos, pos + d, j))(lambda j=j, d=d: shuffle(j, d).start())

    steps = n // 2
    part = block // 2
    lead = 3

    def ring(step, q, way):
        move = 1 if way == 0 else -1
        origin = row_at((pos - move * step + n) % n)
        target = row_at((pos + move + n) % n)
        src = factors.at[q] if step == 0 else full.at[q, origin]
        dst = full.at[q, origin]
        if step == steps - 1:
            cut = pl.ds(way * part, part)
            src, dst = src.at[cut], dst.at[cut]
        return remote(src, dst, l_send.at[way, step, q], l_recv.at[way, step, q], row=target)

    def group(t):
        for step in range(steps - 1, -1, -1):
            q = t - lead * step
            if 0 <= q < vectors:
                for way in range(2):
                    if step > 0:
                        ring(step - 1, q, way).wait_recv()
                    ring(step, q, way).start()

    groups = vectors + lead * (steps - 1)
    ahead = lead * (steps - 1)
    for t in range(min(lead, groups)):
        group(t)

    def own_block(q, _):
        full[q, row] = factors[q]
        return 0

    lax.fori_loop(0, vectors, own_block, 0)

    def passed(h, way):
        return z - h if way == 0 else z + h

    def arrives(h, way):
        return passed(h + 1, way) >= 0 if way == 0 else passed(h + 1, way) < nz

    def leaves(h, way):
        there = passed(h, way) >= 0 if way == 0 else passed(h, way) < nz
        return there & (z + 1 < nz if way == 0 else z > 0)

    def along(j, h, way):
        src = passed(h, way) * 2 + core
        target = (jnp.minimum(z + 1, nz - 1) if way == 0 else jnp.maximum(z - 1, 0)) * 2 + core
        return remote(held.at[j, src], held.at[j, src], t_send.at[j, way, h], t_recv.at[j, way, h], col=target)

    def across(j, h, way):
        src = passed(h, way) * 2 + core
        return remote(held.at[j, src], held.at[j, src], f_send.at[j, way, h], f_recv.at[j, way, h], col=sibling)

    def hop(j, h, way):
        @pl.when(arrives(h - 1, way))
        def _():
            along(j, h - 1, way).wait_recv()
            if h < nz - 1:
                pl.when(leaves(h, way))(lambda: along(j, h, way).start())
            across(j, h, way).start()

    for j in range(WORK):
        for d in shifts:
            pl.when(feasible(pos - d, pos, j))(lambda j=j, d=d: shuffle(j, d).wait_recv())
        src = owner_of(pos * WORK + j) - pos
        chosen = shuf[reach, j]
        for d in shifts:
            chosen = jnp.where(src == d, shuf[d + reach, j], chosen)
        held[j, col] = chosen
        for way in range(2):
            pl.when(leaves(0, way))(lambda j=j, way=way: along(j, 0, way).start())
        across(j, 0, 0).start()

    later = list(range(lead, min(ahead + 2, groups)))
    for h in range(1, nz):
        for j in range(WORK):
            for way in range(2):
                hop(j, h, way)
        if later and h > 1:
            group(later.pop(0))
    for t in later:
        group(t)

    tile = size // 2

    def pair_first(q, j):
        def first(i, _):
            at = pl.ds(pl.multiple_of(i * tile, tile), tile)
            lhs = held.at[j].reshape(size, size)[at, :]
            rhs = full[q].reshape(size, size)
            half[at, :] = lax.dot_general(
                lhs, rhs, (((1,), (1,)), ((), ())), preferred_element_type=jnp.float32).astype(jnp.bfloat16)
            return 0

        lax.fori_loop(0, size // tile, first, 0)

    def pair_second(q, j):
        def second(i, _):
            at = pl.ds(pl.multiple_of(i * tile, tile), tile)
            lhs = full.at[q].reshape(size, size)[at, :]
            value = jnp.dot(lhs, half[...], preferred_element_type=jnp.float32)
            if q == 0:
                acc[j, at, :] = value
            else:
                acc[j, at, :] += value
            return 0

        lax.fori_loop(0, size // tile, second, 0)

    def rows_of(c):
        return pl.ds(pl.multiple_of(c * rows, rows), rows)

    def to_sibling(j):
        return remote(sib_out.at[j], sib_in.at[j], b_send.at[j], b_recv.at[j], col=sibling)

    def to_owner(j, o):
        return remote(z_out.at[j, o], z_in.at[j, o], z_send.at[j, o], z_recv.at[j, o],
                      col=((z + o) % nz) * 2 + core)

    def share(j):
        for k in range(nz):
            sib_out[j, k] = acc[j, rows_of(2 * k + 1 - core), :].astype(jnp.bfloat16)
        to_sibling(j).start()

    def spread(j):
        to_sibling(j).wait_recv()
        for o in range(1, nz):
            k = (z + o) % nz
            total = acc[j, rows_of(2 * k + core), :] + sib_in[j, k].astype(jnp.float32)
            z_out[j, o] = total.astype(jnp.bfloat16)
            to_owner(j, o).start()

    def finish(j):
        rank = pos * WORK + j
        src = owner_of(rank)
        slot = rank - lookup(start_at, src)
        pair = jnp.clip(lookup([row_at(p) for p in range(n)], src) * slots + slot, 0, n * slots - 1)
        energy = occ[pairs[0, pair]] + occ[pairs[1, pair]]
        here = lax.broadcasted_iota(jnp.int32, (rows, size), 0) + col * rows
        there = lax.broadcasted_iota(jnp.int32, (rows, size), 1)
        levels = jnp.broadcast_to(vir[...], (rows, size))
        mine = jnp.sum(jnp.where(here == there, levels, 0.0), axis=1, keepdims=True)
        denominator = mine + levels - energy
        ladder = acc[j, rows_of(col), :] + sib_in[j, z].astype(jnp.float32)
        for o in range(1, nz):
            to_owner(j, o).wait_recv()
            ladder = ladder + z_in[j, o].astype(jnp.float32)
        t = held[j, col].astype(jnp.float32)
        new = t - (ladder + denominator * t) / (denominator + level_shift)
        ret[reach, j] = new.astype(jnp.bfloat16)
        for d in shifts:
            pl.when(feasible(pos + d, pos, j))(lambda j=j, d=d: give_back(j, d).start())

    for q in range(vectors):
        t = q + ahead + 1
        if q > 0 and t < groups:
            group(t)
        for way in range(2):
            ring(steps - 1, q, way).wait_recv()
        for j in range(WORK):
            if q == 0:
                across(j, 0, 0).wait_recv()
                for h in range(1, nz):
                    for way in range(2):
                        pl.when(arrives(h - 1, way))(lambda j=j, h=h, way=way: across(j, h, way).wait_recv())
            pair_first(q, j)
            if q == vectors - 1 and j > 0:
                spread(j - 1)
            pair_second(q, j)
            if q == vectors - 1:
                share(j)
    spread(WORK - 1)
    for j in range(WORK):
        finish(j)
    for j in range(WORK):
        for d in shifts:
            pl.when(feasible(pos, pos + d, j))(lambda j=j, d=d: give_back(j, -d).wait_recv())
    for s in range(slots):
        rank = own_start + s
        where = jnp.clip(rank // WORK - pos + reach, 0, 2 * reach)
        value = ret[where, jnp.clip(rank % WORK, 0, WORK - 1)]
        out[s] = jnp.where(s < own_count, value, jnp.zeros_like(value))

    for j in range(WORK):
        for d in shifts:
            pl.when(feasible(pos, pos + d, j))(lambda j=j, d=d: shuffle(j, d).wait_send())
            pl.when(feasible(pos + d, pos, j))(lambda j=j, d=d: give_back(j, d).wait_send())
        across(j, 0, 0).wait_send()
        for way in range(2):
            for h in range(nz - 1):
                pl.when(leaves(h, way))(lambda j=j, h=h, way=way: along(j, h, way).wait_send())
                pl.when(arrives(h, way))(lambda j=j, h=h, way=way: across(j, h + 1, way).wait_send())
        for o in range(1, nz):
            to_owner(j, o).wait_send()
        to_sibling(j).wait_send()
    for q in range(vectors):
        for step in range(steps):
            for way in range(2):
                ring(step, q, way).wait_send()


def solution(mesh):
    n, m = mesh.shape["row"], mesh.shape["col"]

    def per_device(amplitudes, factors, counts, pair_index, occ_energy, vir_energy):
        slots, rows, size = amplitudes.shape
        vectors, block, _ = factors.shape
        reach = reach_of(n, slots)
        span, nz, steps = 2 * reach + 1, m // 2, n // 2
        bf16, f32 = jnp.bfloat16, jnp.float32
        dma = pltpu.SemaphoreType.DMA
        vmem, smem = pl.BlockSpec(memory_space=pltpu.VMEM), pl.BlockSpec(memory_space=pltpu.SMEM)
        flops = 4 * vectors * WORK * size ** 3
        return pl.pallas_call(
            functools.partial(kernel, n, m, reach),
            out_shape=jax.ShapeDtypeStruct((slots, rows, size), bf16),
            in_specs=[vmem, vmem, smem, smem, smem, vmem],
            out_specs=vmem,
            scratch_shapes=[
                pltpu.VMEM((vectors, n, block, size), bf16),
                pltpu.VMEM((WORK, m, rows, size), bf16),
                pltpu.VMEM((size, size), bf16),
                pltpu.VMEM((WORK, size, size), f32),
                pltpu.VMEM((span, WORK, rows, size), bf16),
                pltpu.VMEM((span, WORK, rows, size), bf16),
                pltpu.VMEM((WORK, nz, rows, size), bf16),
                pltpu.VMEM((WORK, nz, rows, size), bf16),
                pltpu.VMEM((WORK, nz, rows, size), bf16),
                pltpu.VMEM((WORK, nz + 1, rows, size), bf16),
                pltpu.VMEM((span, WORK, rows, size), bf16),
                dma((2, steps, vectors)), dma((2, steps, vectors)),
                dma((span, WORK)), dma((span, WORK)),
                dma((WORK, 2, nz)), dma((WORK, 2, nz)),
                dma((WORK, 2, nz)), dma((WORK, 2, nz)),
                dma((WORK,)), dma((WORK,)),
                dma((WORK, nz)), dma((WORK, nz + 1)),
                dma((span, WORK)), dma((span, WORK)),
            ],
            cost_estimate=pl.CostEstimate(flops=flops, bytes_accessed=2 * vectors * size * size, transcendentals=0),
            compiler_params=pltpu.CompilerParams(
                collective_id=0, has_side_effects=True, vmem_limit_bytes=56 * 2 ** 20),
        )(amplitudes, factors, counts, pair_index.T, occ_energy, vir_energy)

    in_specs = (P("row", "col", None), P("col", "row", None), P(), P(), P(), P())
    return jax.shard_map(
        per_device, mesh=mesh, in_specs=in_specs, out_specs=P("row", "col", None), check_vma=False)
```

```python
import functools

import jax
import jax.numpy as jnp
from jax import lax
from jax.experimental import pallas as pl
from jax.experimental.pallas import tpu as pltpu
from jax.sharding import PartitionSpec as P

WORK = 2
level_shift = 1.0
MESH = pl.DeviceIdType.MESH


def rank_range(pos, n, slots):
    total = WORK * n
    if isinstance(pos, int):
        return max(pos, total - slots * (n - pos)), min(slots * (pos + 1), total - (n - pos - 1))
    low = jnp.maximum(pos, total - slots * (n - pos))
    high = jnp.minimum(slots * (pos + 1), total - (n - pos - 1))
    return low, high


def reach_of(n, slots):
    reach = 0
    for pos in range(n):
        low, high = rank_range(pos, n, slots)
        reach = max([reach] + [abs(k // WORK - pos) for k in range(low, high)])
    return reach


def kernel(n, m, reach, amps, factors, counts, pairs, occ, vir, out,
           full, held, half, acc, stage, shuf, sib_out, sib_in, z_out, z_in, ret,
           l_send, l_recv, s_send, s_recv, t_send, t_recv, f_send, f_recv,
           b_send, b_recv, z_send, z_recv, r_send, r_recv):
    slots, rows, size = amps.shape
    vectors, block = factors.shape[0], factors.shape[1]
    nz = m // 2
    row, col = lax.axis_index("row"), lax.axis_index("col")
    z, core = col // 2, col % 2
    sibling = z * 2 + 1 - core
    pos = row // 2 + (row % 2) * (n - 1 - 2 * (row // 2))

    def row_at(p):
        if isinstance(p, int):
            return 2 * p if p < n // 2 else 2 * (n - 1 - p) + 1
        back = p // (n // 2)
        return (1 - back) * 2 * p + back * (2 * (n - 1 - p) + 1)

    def remote(src, dst, send, recv, **where):
        return pltpu.make_async_remote_copy(
            src_ref=src, dst_ref=dst, send_sem=send, recv_sem=recv, device_id=where, device_id_type=MESH)

    barrier = pltpu.get_barrier_semaphore()
    for step in range(1, n):
        pl.semaphore_signal(barrier, inc=1, device_id={"row": (row + step) % n}, device_id_type=MESH)
    for step in range(1, m):
        pl.semaphore_signal(barrier, inc=1, device_id={"col": (col + step) % m}, device_id_type=MESH)

    count_at = [counts[row_at(p)] for p in range(n)]
    start_at, running = [], jnp.int32(0)
    for p in range(n):
        start_at.append(running)
        running = running + count_at[p]

    def lookup(values, p):
        found = jnp.int32(0)
        for i in range(n):
            found = jnp.where(p == i, values[i], found)
        return found

    own_start, own_count = lookup(start_at, pos), lookup(count_at, pos)

    def owner_of(rank):
        src = jnp.int32(0)
        for p in range(n - 1):
            src = src + jnp.where(start_at[p] + count_at[p] <= rank, 1, 0)
        return src

    def feasible(p, worker, j):
        low, high = rank_range(p, n, slots)
        rank = worker * WORK + j
        return (p >= 0) & (p < n) & (worker >= 0) & (worker < n) & (rank >= low) & (rank < high)

    shifts = [d for d in range(-reach, reach + 1) if d != 0]
    for j in range(WORK):
        for d in shifts:
            slot = jnp.clip((pos + d) * WORK + j - own_start, 0, slots - 1)
            stage[d + reach, j] = amps[slot]
        shuf[reach, j] = amps[jnp.clip(pos * WORK + j - own_start, 0, slots - 1)]

    pl.semaphore_wait(barrier, n + m - 2)

    def shuffle(j, d):
        target = row_at((pos + d + n) % n)
        return remote(stage.at[d + reach, j], shuf.at[reach - d, j], s_send.at[d + reach, j], s_recv.at[reach - d, j],
                      row=target)

    def give_back(j, d):
        target = row_at((pos + d + n) % n)
        return remote(ret.at[reach, j], ret.at[reach - d, j], r_send.at[d + reach, j], r_recv.at[reach - d, j],
                      row=target)

    for j in range(WORK):
        for d in shifts:
            pl.when(feasible(pos, pos + d, j))(lambda j=j, d=d: shuffle(j, d).start())

    steps = n // 2
    part = block // 2
    lead = 2

    def ring(step, q, way):
        move = 1 if way == 0 else -1
        origin = row_at((pos - move * step + n) % n)
        target = row_at((pos + move + n) % n)
        src = factors.at[q] if step == 0 else full.at[q, origin]
        dst = full.at[q, origin]
        if step == steps - 1:
            cut = pl.ds(way * part, part)
            src, dst = src.at[cut], dst.at[cut]
        return remote(src, dst, l_send.at[way, step, q], l_recv.at[way, step, q], row=target)

    def group(t):
        for step in range(steps - 1, -1, -1):
            q = t - lead * step
            if 0 <= q < vectors:
                for way in range(2):
                    if step > 0:
                        ring(step - 1, q, way).wait_recv()
                    ring(step, q, way).start()

    groups = vectors + lead * (steps - 1)
    ahead = lead * (steps - 1)
    for t in range(min(lead, groups)):
        group(t)

    def own_block(q, _):
        full[q, row] = factors[q]
        return 0

    lax.fori_loop(0, vectors, own_block, 0)

    def along(j, o):
        return remote(held.at[j, col], held.at[j, col], t_send.at[j, o], t_recv.at[j, o],
                      col=((z + o) % nz) * 2 + core)

    def across(j, o):
        from_z = (z - o + nz) % nz
        src = from_z * 2 + core
        return remote(held.at[j, src], held.at[j, src], f_send.at[j, o], f_recv.at[j, o], col=sibling)

    for j in range(WORK):
        for d in shifts:
            pl.when(feasible(pos - d, pos, j))(lambda j=j, d=d: shuffle(j, d).wait_recv())
        src = owner_of(pos * WORK + j) - pos
        chosen = shuf[reach, j]
        for d in shifts:
            chosen = jnp.where(src == d, shuf[d + reach, j], chosen)
        held[j, col] = chosen
        for o in range(1, nz):
            along(j, o).start()
        across(j, 0).start()

    for t in range(2, min(ahead + 1, groups)):
        group(t)
    for j in range(WORK):
        for o in range(1, nz):
            along(j, o).wait_recv()
            across(j, o).start()
    if ahead + 1 < groups:
        group(ahead + 1)

    tile = size // 2

    def pair_first(q, j):
        def first(i, _):
            at = pl.ds(pl.multiple_of(i * tile, tile), tile)
            lhs = held.at[j].reshape(size, size)[at, :]
            rhs = full[q].reshape(size, size)
            half[at, :] = lax.dot_general(
                lhs, rhs, (((1,), (1,)), ((), ())), preferred_element_type=jnp.float32).astype(jnp.bfloat16)
            return 0

        lax.fori_loop(0, size // tile, first, 0)

    def pair_second(q, j):
        def second(i, _):
            at = pl.ds(pl.multiple_of(i * tile, tile), tile)
            lhs = full.at[q].reshape(size, size)[at, :]
            value = jnp.dot(lhs, half[...], preferred_element_type=jnp.float32)
            if q == 0:
                acc[j, at, :] = value
            else:
                acc[j, at, :] += value
            return 0

        lax.fori_loop(0, size // tile, second, 0)

    def rows_of(c):
        return pl.ds(pl.multiple_of(c * rows, rows), rows)

    def to_sibling(j):
        return remote(sib_out.at[j], sib_in.at[j], b_send.at[j], b_recv.at[j], col=sibling)

    def onward(j, k, way):
        target = (jnp.minimum(z + 1, nz - 1) if way == 0 else jnp.maximum(z - 1, 0)) * 2 + core
        slot = k if way == 0 else jnp.where(k == z - 1, nz, k)
        return remote(z_out.at[j, k], z_in.at[j, slot], z_send.at[j, k], z_recv.at[j, slot], col=target)

    def incoming(j, slot):
        sent = min(slot, nz - 1) if isinstance(slot, int) else slot
        return remote(z_out.at[j, sent], z_in.at[j, slot], z_send.at[j, sent], z_recv.at[j, slot], col=sibling)

    def share(j):
        for k in range(nz):
            sib_out[j, k] = acc[j, rows_of(2 * k + 1 - core), :].astype(jnp.bfloat16)
        to_sibling(j).start()

    def chain(j, action):
        def one_way(way):
            for i in range(nz - 1):
                k = nz - 1 - i if way == 0 else i
                ahead_of = (k > z) if way == 0 else (k < z)
                first = (z == 0) if way == 0 else (z == nz - 1)
                action(j, k, way, ahead_of, first)

        low = z < nz // 2
        pl.when(low)(lambda: one_way(0))
        one_way(1)
        pl.when(jnp.logical_not(low))(lambda: one_way(0))

    def begin(j, k, way, ahead_of, first):
        @pl.when(ahead_of & first)
        def _():
            total = acc[j, rows_of(2 * k + core), :] + sib_in[j, k].astype(jnp.float32)
            z_out[j, k] = total.astype(jnp.bfloat16)
            onward(j, k, way).start()

    def go_on(j, k, way, ahead_of, first):
        @pl.when(ahead_of & jnp.logical_not(first))
        def _():
            total = acc[j, rows_of(2 * k + core), :] + sib_in[j, k].astype(jnp.float32)
            incoming(j, k).wait_recv()
            z_out[j, k] = (total + z_in[j, k].astype(jnp.float32)).astype(jnp.bfloat16)
            onward(j, k, way).start()

    def spread(j):
        to_sibling(j).wait_recv()
        chain(j, begin)

    def finish(j):
        rank = pos * WORK + j
        src = owner_of(rank)
        slot = rank - lookup(start_at, src)
        pair = jnp.clip(lookup([row_at(p) for p in range(n)], src) * slots + slot, 0, n * slots - 1)
        energy = occ[pairs[0, pair]] + occ[pairs[1, pair]]
        here = lax.broadcasted_iota(jnp.int32, (rows, size), 0) + col * rows
        there = lax.broadcasted_iota(jnp.int32, (rows, size), 1)
        levels = jnp.broadcast_to(vir[...], (rows, size))
        mine = jnp.sum(jnp.where(here == there, levels, 0.0), axis=1, keepdims=True)
        denominator = mine + levels - energy
        own = rows_of(col)
        acc[j, own, :] += sib_in[j, z].astype(jnp.float32)

        @pl.when(z > 0)
        def _():
            incoming(j, z).wait_recv()
            acc[j, own, :] += z_in[j, z].astype(jnp.float32)

        @pl.when(z < nz - 1)
        def _():
            incoming(j, nz).wait_recv()
            acc[j, own, :] += z_in[j, nz].astype(jnp.float32)

        ladder = acc[j, own, :]
        t = held[j, col].astype(jnp.float32)
        new = t - (ladder + denominator * t) / (denominator + level_shift)
        ret[reach, j] = new.astype(jnp.bfloat16)
        for d in shifts:
            pl.when(feasible(pos + d, pos, j))(lambda j=j, d=d: give_back(j, d).start())

    for q in range(vectors):
        t = q + ahead + 1
        if q > 0 and t < groups:
            group(t)
        for way in range(2):
            ring(steps - 1, q, way).wait_recv()
        for j in range(WORK):
            if q == 0:
                for o in range(nz):
                    across(j, o).wait_recv()
            pair_first(q, j)
            if q == vectors - 1 and j > 0:
                spread(j - 1)
            pair_second(q, j)
            if q == vectors - 1:
                share(j)
    for j in range(WORK - 1):
        chain(j, go_on)
    spread(WORK - 1)
    for j in range(WORK - 1):
        finish(j)
    chain(WORK - 1, go_on)
    finish(WORK - 1)
    for j in range(WORK):
        for d in shifts:
            pl.when(feasible(pos, pos + d, j))(lambda j=j, d=d: give_back(j, -d).wait_recv())
    for s in range(slots):
        rank = own_start + s
        where = jnp.clip(rank // WORK - pos + reach, 0, 2 * reach)
        value = ret[where, jnp.clip(rank % WORK, 0, WORK - 1)]
        out[s] = jnp.where(s < own_count, value, jnp.zeros_like(value))

    for j in range(WORK):
        for d in shifts:
            pl.when(feasible(pos, pos + d, j))(lambda j=j, d=d: shuffle(j, d).wait_send())
            pl.when(feasible(pos + d, pos, j))(lambda j=j, d=d: give_back(j, d).wait_send())
        for o in range(1, nz):
            along(j, o).wait_send()
        for o in range(nz):
            across(j, o).wait_send()
        for k in range(nz):
            pl.when(z != k)(lambda j=j, k=k: incoming(j, k).wait_send())
        to_sibling(j).wait_send()
    for q in range(vectors):
        for step in range(steps):
            for way in range(2):
                ring(step, q, way).wait_send()


def solution(mesh):
    n, m = mesh.shape["row"], mesh.shape["col"]

    def per_device(amplitudes, factors, counts, pair_index, occ_energy, vir_energy):
        slots, rows, size = amplitudes.shape
        vectors, block, _ = factors.shape
        reach = reach_of(n, slots)
        span, nz, steps = 2 * reach + 1, m // 2, n // 2
        bf16, f32 = jnp.bfloat16, jnp.float32
        dma = pltpu.SemaphoreType.DMA
        vmem, smem = pl.BlockSpec(memory_space=pltpu.VMEM), pl.BlockSpec(memory_space=pltpu.SMEM)
        flops = 4 * vectors * WORK * size ** 3
        return pl.pallas_call(
            functools.partial(kernel, n, m, reach),
            out_shape=jax.ShapeDtypeStruct((slots, rows, size), bf16),
            in_specs=[vmem, vmem, smem, smem, smem, vmem],
            out_specs=vmem,
            scratch_shapes=[
                pltpu.VMEM((vectors, n, block, size), bf16),
                pltpu.VMEM((WORK, m, rows, size), bf16),
                pltpu.VMEM((size, size), bf16),
                pltpu.VMEM((WORK, size, size), f32),
                pltpu.VMEM((span, WORK, rows, size), bf16),
                pltpu.VMEM((span, WORK, rows, size), bf16),
                pltpu.VMEM((WORK, nz, rows, size), bf16),
                pltpu.VMEM((WORK, nz, rows, size), bf16),
                pltpu.VMEM((WORK, nz, rows, size), bf16),
                pltpu.VMEM((WORK, nz + 1, rows, size), bf16),
                pltpu.VMEM((span, WORK, rows, size), bf16),
                dma((2, steps, vectors)), dma((2, steps, vectors)),
                dma((span, WORK)), dma((span, WORK)),
                dma((WORK, nz)), dma((WORK, nz)),
                dma((WORK, nz)), dma((WORK, nz)),
                dma((WORK,)), dma((WORK,)),
                dma((WORK, nz)), dma((WORK, nz + 1)),
                dma((span, WORK)), dma((span, WORK)),
            ],
            cost_estimate=pl.CostEstimate(flops=flops, bytes_accessed=2 * vectors * size * size, transcendentals=0),
            compiler_params=pltpu.CompilerParams(
                collective_id=0, has_side_effects=True, vmem_limit_bytes=56 * 2 ** 20),
        )(amplitudes, factors, counts, pair_index.T, occ_energy, vir_energy)

    in_specs = (P("row", "col", None), P("col", "row", None), P(), P(), P(), P())
    return jax.shard_map(
        per_device, mesh=mesh, in_specs=in_specs, out_specs=P("row", "col", None), check_vma=False)
```
